32 devices in a mesh: energy: 4 (over y, x), slab: 8 (over z, core).
Axes of the slice: x: 2, y: 2, z: 4, core: 2. Of those that a mesh axis runs over, the one named last changes fastest.
Arguments:
- greens: bfloat16 [2, 8, 32, 128, 256], P(None, 'energy', 'slab'), may hold values from -6 to 6
- coupling: bfloat16 [4, 3, 128, 128], replicated, may hold values from -0.15625 to 0.15625
- occupation: float32 [4], replicated, may hold values from 0.2 to 3
- offsets: int32 [4], replicated, may hold values from 1 to 2, as said below
- neighbours: int32 [32, 3], P('slab'), may hold values from -1 to 31, as said below
Outputs:
- sigma: bfloat16 [2, 8, 32, 128, 256], P(None, 'energy', 'slab')
The draws below stay inside these ranges and needn't reach their ends.
Inputs may be any that keep to these rules, and one draw needn't show every extreme that they name: `offsets`: every offset is 1 to 2; one mode has offset 2 and one has offset 1. `neighbours`: an entry is -1 (padding) or an atom block that differs from the row's own block by at most 1. Block a with a % 4 == 0 and a > 0 lists a - 1 in slot 1; block a with a % 4 == 3 and a < 31 lists a + 1 in slot 2.
All inputs are finite; a program needn't handle non-finite values.
Results may differ from the reference program's by a relative error of at most 0.0058.
Values may be sent and summed in bfloat16 or wider, within the bound.
No kernel may reach another device: no remote copies, remote signals or barrier semaphores. Data moves between devices by JAX's collectives and lax.ppermute only.
A program may use at most 128 MiB of HBM per device.

```python
import math
import jax
import jax.numpy as jnp
from jax import lax

NO = 128
NM = 4
K = 3
NE_DEV = 2
NB_DEV = 4
NE = 8
NB = 32


def draw_offsets(key, part):
    key = jax.random.fold_in(key, 11)
    first_key, second_key = jax.random.split(key)
    values_drawn = jax.random.randint(first_key, (NM,), 1, NE_DEV + 1)
    chosen = jax.random.permutation(second_key, NM)
    values_drawn = values_drawn.at[chosen[0]].set(NE_DEV)
    values_drawn = values_drawn.at[chosen[1]].set(1)
    return values_drawn.astype(jnp.int32)


def draw_neighbours(key, part):
    key = jax.random.fold_in(key, 23)
    first_key, second_key = jax.random.split(key)
    stride = jax.random.randint(first_key, (NB, K), -1, 2)
    is_live = jax.random.randint(second_key, (NB, K), 0, 10) < 7
    row_ids = jnp.arange(NB, dtype=jnp.int32)[:, None]
    target = row_ids + stride
    usable = is_live & (target >= 0) & (target < NB)
    listed = jnp.where(usable, target, -1)
    listed = listed.at[NB - 1, 0].set(NB - 1)
    listed = listed.at[0, 0].set(-1)
    row_flat = jnp.arange(NB, dtype=jnp.int32)
    place = row_flat % NB_DEV
    before_col = jnp.where((place == 0) & (row_flat > 0), row_flat - 1, listed[:, 1])
    after_col = jnp.where((place == NB_DEV - 1) & (row_flat < NB - 1), row_flat + 1, listed[:, 2])
    listed = listed.at[:, 1].set(before_col)
    listed = listed.at[:, 2].set(after_col)
    return listed.astype(jnp.int32)


def block_scale(stream_key, extent, cuts, least, high):
    def one(dim, blocks):
        steps = jax.random.uniform(jax.random.fold_in(jax.random.fold_in(stream_key, 6), dim), (blocks,), jnp.float32, least / len(cuts), high / len(cuts))
        return jnp.repeat(jnp.exp(steps), extent[dim] // blocks).reshape((-1,) + (1,) * (len(extent) - dim - 1))

    loudness = one(*cuts[0])
    for cut in cuts[1:]:
        loudness = loudness * one(*cut)
    return loudness


def bell_draw(stream_key, dims, spread, most, shards=(), kind=jnp.bfloat16):
    entries = jax.random.normal(stream_key, dims, jnp.float32) * spread
    if len(shards) > 0:
        entries = block_scale(stream_key, dims, shards, -0.22, 0.18) * entries
    return jnp.clip(entries, min=-most, max=most).astype(kind)


def setup_inputs(seed: int = 0) -> dict:
    key_of = jax.random.split(jax.random.key(seed), 6)
    return {
        "greens": bell_draw(key_of[0], (2, NE, NB, NO, 2 * NO), 1.0, 6.0, ((1, 4), (2, 8))),
        "coupling": bell_draw(key_of[1], (NM, K, NO, NO), (NO * NM * K) ** -0.5, 0.15625),
        "occupation": jnp.clip(jnp.exp(jax.random.uniform(key_of[2], (NM,), jnp.float32, math.log(0.2), math.log(3.0))), 0.2, 3.0),
        "offsets": draw_offsets(jax.random.fold_in(key_of[5], 71), 0),
        "neighbours": draw_neighbours(jax.random.fold_in(key_of[5], 71), 0),
    }


def couple(blocks, matrix):
    half = jnp.einsum("pq,...qr->...pr", matrix.astype(jnp.float32), blocks.astype(jnp.float32)).astype(jnp.bfloat16)
    shaped = half.reshape(half.shape[:-1] + (2, half.shape[-1] // 2))
    result = jnp.einsum("...psq,rq->...psr", shaped.astype(jnp.float32), matrix.astype(jnp.float32))
    return result.reshape(blocks.shape)


def reference(greens, coupling, occupation, offsets, neighbours):
    is_live = neighbours >= 0
    source = jnp.where(is_live, neighbours, 0).astype(jnp.int32)

    def one_energy(energy):
        summed = jnp.zeros((2, NB, NO, 2 * NO), jnp.float32)
        for mode_at in range(NM):
            filling = occupation[mode_at]
            shift_by = offsets[mode_at]
            ahead = lax.dynamic_index_in_dim(greens, ((energy + shift_by) % NE).astype(jnp.int32), 1, keepdims=False).astype(jnp.float32)
            behind = lax.dynamic_index_in_dim(greens, ((energy - shift_by) % NE).astype(jnp.int32), 1, keepdims=False).astype(jnp.float32)
            lesser = (filling + 1.0) * ahead[0] + filling * behind[0]
            greater = (filling + 1.0) * behind[1] + filling * ahead[1]
            mixture = jnp.stack([lesser, greater]).astype(jnp.bfloat16)
            for slot_at in range(K):
                picked = jnp.take(mixture, source[:, slot_at], axis=1)
                picked = jnp.where(is_live[None, :, slot_at, None, None], picked, jnp.zeros((), jnp.bfloat16))
                summed = summed + couple(picked, coupling[mode_at, slot_at])
        return summed.astype(jnp.bfloat16)

    stacked = lax.map(one_energy, jnp.arange(NE, dtype=jnp.int32))
    return jnp.transpose(stacked, (1, 0, 2, 3, 4))
```

```python
import functools

import jax
import jax.numpy as jnp
from jax import lax
from jax.experimental import pallas as pl
from jax.experimental.pallas import tpu as pltpu
from jax.sharding import PartitionSpec as P


def partial_body(part, blocks, halo, *refs):
    if halo:
        occ, off, nbr, c_ref, g_ref, b_ref, a_ref = refs[:7]
    else:
        occ, off, nbr, c_ref, g_ref = refs[:5]
    far, near, mine, rows, cols, half, acc = refs[-7:]
    modes, slots, size = c_ref.shape[:3]
    count = g_ref.shape[1]
    owned = nbr.shape[0]
    first = lax.axis_index("slab") * owned
    odd = lax.rem(lax.axis_index("energy"), 2)
    for m in range(modes):
        for k in range(slots):
            c = c_ref[m, k]
            rows[k, m * size : (m + 1) * size, :] = c
            cols[m, :, k * size : (k + 1) * size] = c

    def per_block(i, carry):
        a = blocks[0] + (blocks[-1] - blocks[0]) * i
        acc[...] = jnp.zeros_like(acc)
        for e in range(count):
            for k in range(slots):
                v = nbr[a, k]
                at = v - first
                src = g_ref[0, e, jnp.clip(at, 0, owned - 1)]
                if halo:
                    src = jnp.where(at < 0, b_ref[0, e, 0], src)
                    src = jnp.where(at >= owned, a_ref[0, e, 0], src)
                src = jnp.where(v >= 0, src, jnp.zeros_like(src))
                r = jnp.dot(rows[k], src, preferred_element_type=jnp.float32)
                r = r.astype(jnp.bfloat16)
                for m in range(modes):
                    for s in range(2):
                        h = (e * 2 + s) * size
                        half[m, h : h + size, k * size : (k + 1) * size] = r[
                            m * size : (m + 1) * size, s * size : (s + 1) * size
                        ]
        for m in range(modes):
            y = lax.dot_general(
                half[m], cols[m], (((1,), (1,)), ((), ())), preferred_element_type=jnp.float32
            )
            o = off[m]
            n = occ[m]
            down, up = (n + 1.0, n) if part == 0 else (n, n + 1.0)
            for e in range(count):
                for s in range(2):
                    h = (e * 2 + s) * size
                    ys = y[h : h + size]
                    acc[e - o + count, :, s * size : (s + 1) * size] += down * ys
                    acc[e + o + count, :, s * size : (s + 1) * size] += up * ys
        for j in range(count):
            far[0, j, i] = acc[2 * count * odd + j].astype(jnp.bfloat16)
            near[0, j, i] = acc[2 * count * (1 - odd) + j]
            mine[0, j, i] = acc[count + j]
        return carry

    lax.fori_loop(0, len(blocks), per_block, 0)


def whole(shape):
    return pl.BlockSpec(shape, lambda i: (0,) * len(shape))


def partial(part, blocks, greens, coupling, occupation, offsets, neighbours, edges=()):
    specs = [pl.BlockSpec(memory_space=pltpu.SMEM)] * 3 + [whole(coupling.shape)]
    for array in (greens,) + tuple(edges):
        specs.append(pl.BlockSpec((1,) + array.shape[1:], lambda i: (part, 0, 0, 0, 0)))
    modes, slots, size = coupling.shape[:3]
    count = greens.shape[1]
    n = len(blocks)
    shape = (1, count, n) + greens.shape[3:]
    return pl.pallas_call(
        functools.partial(partial_body, part, blocks, len(edges) > 0),
        out_shape=[
            jax.ShapeDtypeStruct(shape, jnp.bfloat16),
            jax.ShapeDtypeStruct(shape, jnp.float32),
            jax.ShapeDtypeStruct(shape, jnp.float32),
        ],
        grid=(1,),
        in_specs=specs,
        out_specs=[whole(shape)] * 3,
        scratch_shapes=[
            pltpu.VMEM((slots, modes * size, size), jnp.bfloat16),
            pltpu.VMEM((modes, size, slots * size), jnp.bfloat16),
            pltpu.VMEM((modes, count * 2 * size, slots * size), jnp.bfloat16),
            pltpu.VMEM((3 * count, size, 2 * size), jnp.float32),
        ],
        compiler_params=pltpu.CompilerParams(vmem_limit_bytes=32 << 20),
        cost_estimate=pl.CostEstimate(
            flops=8 * count * n * modes * slots * size * size * size,
            bytes_accessed=4 << 20,
            transcendentals=0,
        ),
    )(occupation, offsets, neighbours, coupling, greens, *edges)


def finish_body(mine, received, *refs):
    out = refs[-1]
    out[...] = (mine[...] + received[...].astype(jnp.float32)).astype(jnp.bfloat16)


def finish(part, blocks, mine, received, shape, out):
    block = (1, mine.shape[1], 1) + mine.shape[3:]
    spec = pl.BlockSpec(block, lambda i: (0, 0, i, 0, 0))
    step = blocks[-1] - blocks[0]
    return pl.pallas_call(
        finish_body,
        out_shape=jax.ShapeDtypeStruct(shape, jnp.bfloat16),
        grid=(len(blocks),),
        in_specs=[spec, spec] + ([pl.BlockSpec(memory_space=pl.ANY)] if out is not None else []),
        out_specs=pl.BlockSpec(block, lambda i: (part, 0, blocks[0] + i * step, 0, 0)),
        input_output_aliases={2: 0} if out is not None else {},
        cost_estimate=pl.CostEstimate(flops=mine.size, bytes_accessed=8 * mine.size, transcendentals=0),
    )(mine, received, *([out] if out is not None else []))


def on_device(greens, coupling, occupation, offsets, neighbours):
    slabs = lax.axis_size("slab")
    owned = greens.shape[2]
    across = [(i, i ^ 1) for i in range(4)]
    along = [(i, i ^ 2) for i in range(4)]
    upward = [(i, i + 1) for i in range(slabs - 1)]
    downward = [(i + 1, i) for i in range(slabs - 1)]
    before = lax.ppermute(greens[:, :, owned - 1 :], "slab", upward)
    after = lax.ppermute(greens[:, :, :1], "slab", downward)
    inner, outer = tuple(range(1, owned - 1)), (0, owned - 1)
    chunks = [(1, inner), (0, inner), (1, outer), (0, outer)]
    args = (greens, coupling, occupation, offsets, neighbours)
    pieces = []
    for part, blocks in chunks:
        edges = (before, after) if blocks == outer else ()
        far, near, mine = partial(part, blocks, *args, edges)
        pieces.append((near, mine, lax.ppermute(far, "energy", along)))
    out = None
    for (part, blocks), (near, mine, relayed) in zip(chunks, pieces):
        both = (near + relayed.astype(jnp.float32)).astype(jnp.bfloat16)
        received = lax.ppermute(both, "energy", across)
        out = finish(part, blocks, mine, received, greens.shape, out)
    return out


def solution(mesh):
    in_specs = (P(None, "energy", "slab", None, None), P(), P(), P(), P("slab", None))
    out_specs = P(None, "energy", "slab", None, None)
    return jax.shard_map(
        on_device, mesh=mesh, in_specs=in_specs, out_specs=out_specs, check_vma=False
    )
```

```python
import functools

import jax
import jax.numpy as jnp
from jax import lax
from jax.experimental import pallas as pl
from jax.experimental.pallas import tpu as pltpu
from jax.sharding import PartitionSpec as P

BF16 = jnp.bfloat16
F32 = jnp.float32


def stack_coupling(c_ref, rows, cols):
    modes, slots, size = c_ref.shape[:3]
    for m in range(modes):
        for k in range(slots):
            c = c_ref[m, k]
            rows[k, m * size : (m + 1) * size, :] = c
            cols[m, :, k * size : (k + 1) * size] = c


def source_tile(nbr, first, owned, at, e, k, own, edges):
    listed = nbr[at, k]
    local = listed - first
    tile = own[e, jnp.clip(local, 0, owned - 1)]
    if edges:
        tile = jnp.where(local < 0, edges[0][e, 0], tile)
        tile = jnp.where(local >= owned, edges[1][e, 0], tile)
    return jnp.where(listed >= 0, tile, jnp.zeros_like(tile))


def terms(part, blocks, flip, occ, off, nbr, rows, cols, own, edges, outs, half, acc):
    far, near, mine = outs
    slots, wide, size = rows.shape
    modes = wide // size
    count, owned, _, lanes = own.shape
    per = 2 * size // lanes
    first = lax.axis_index("slab") * owned
    odd = lax.rem(lax.axis_index("energy") + flip, 2)
    step = blocks[1] - blocks[0]

    def group(i, carry):
        if per == 1:
            places = [(blocks[0] + step * i, i)]
        elif len(blocks) == 2:
            places = [(blocks[0], 0), (blocks[1], 1)]
        else:
            places = [(2 * i, 2 * i), (2 * i + 1, 2 * i + 1)]
        acc[...] = jnp.zeros_like(acc)
        for k in range(slots):
            for j in range(2):
                if per == 1:
                    src = source_tile(nbr, first, owned, places[0][0], j, k, own, edges)
                else:
                    src = jnp.concatenate(
                        [source_tile(nbr, first, owned, places[j][0], e, k, own, edges) for e in range(count)],
                        axis=1,
                    )
                r = jnp.dot(rows[k], src, preferred_element_type=F32).astype(BF16)
                for m in range(modes):
                    for h in range(2):
                        e, u = (j, h) if per == 1 else (h, j)
                        to = (e * 2 + u) * size
                        half[m, to : to + size, k * size : (k + 1) * size] = r[
                            m * size : (m + 1) * size, h * size : (h + 1) * size
                        ]

        def second(m):
            y = lax.dot_general(
                half[m], cols[m], (((1,), (1,)), ((), ())), preferred_element_type=F32
            )
            o = off[m]
            n = occ[m]
            down, up = (n + 1.0, n) if part == 0 else (n, n + 1.0)
            for e in range(count):
                for u in range(2):
                    to = (e * 2 + u) * size
                    ys = y[to : to + size]
                    acc[e - o + count, u] += down * ys
                    acc[e + o + count, u] += up * ys

        for m in range(modes):
            if far is None and near is None:
                pl.when(off[m] < count)(functools.partial(second, m))
            else:
                second(m)
        for j in range(count):
            for u in range(2):
                to, cut = (places[0][1], slice(u * size, (u + 1) * size)) if per == 1 else (places[u][1], slice(0, size))
                if far is not None:
                    far[0, j, to, :, cut] = acc[2 * count * odd + j, u].astype(BF16)
                if near is not None:
                    near[0, j, to, :, cut] = acc[2 * count * (1 - odd) + j, u]
                if mine is not None:
                    mine[0, j, to, :, cut] = acc[count + j, u]
        return carry

    groups = len(blocks) // per
    if groups == 1:
        group(0, 0)
    else:
        lax.fori_loop(0, groups, group, 0)


def scratch(modes, slots, size, count):
    return [
        pltpu.VMEM((modes, count * 2 * size, slots * size), BF16),
        pltpu.VMEM((3 * count, 2, size, size), F32),
    ]


def first_body(part, blocks, occ_h, off_h, nbr_h, c_h, g_h, far, near, mine, rows, cols, raw, last, head, occ, off, nbr, c_ref, own, sems, half, acc):
    size = c_h.shape[-1]
    owned = g_h.shape[2]
    copies = [
        pltpu.make_async_copy(src, dst, sems.at[i])
        for i, (src, dst) in enumerate(
            [
                (c_h, c_ref),
                (g_h.at[part], own),
                (occ_h, occ),
                (off_h, off),
                (nbr_h, nbr),
                (g_h.at[pl.ds(1 - part, 1), :, :, :, pl.ds(0, size)], raw),
                (g_h.at[:, :, pl.ds(owned - 1, 1)], last),
                (g_h.at[:, :, pl.ds(0, 1)], head),
            ]
        )
    ]
    for copy in copies:
        copy.start()
    copies[0].wait()
    stack_coupling(c_ref, rows, cols)
    for copy in copies[1:5]:
        copy.wait()
    terms(part, blocks, 0, occ, off, nbr, rows, cols, own, (), (far, near, mine), half, acc)
    for copy in copies[5:]:
        copy.wait()


def first_call(part, blocks, greens, coupling, occupation, offsets, neighbours):
    modes, slots, size = coupling.shape[:3]
    parts, count, owned = greens.shape[:3]
    shape = (1, count, len(blocks), size, 2 * size)
    edge = (parts, count, 1, size, 2 * size)
    anywhere = pl.BlockSpec(memory_space=pl.ANY)
    vmem = pl.BlockSpec(memory_space=pltpu.VMEM)
    return pl.pallas_call(
        functools.partial(first_body, part, blocks),
        out_shape=[
            jax.ShapeDtypeStruct(shape, BF16),
            jax.ShapeDtypeStruct(shape, F32),
            jax.ShapeDtypeStruct(shape, F32),
            jax.ShapeDtypeStruct((slots, modes * size, size), BF16),
            jax.ShapeDtypeStruct((modes, size, slots * size), BF16),
            jax.ShapeDtypeStruct((1, count, owned, size, size), BF16),
            jax.ShapeDtypeStruct(edge, BF16),
            jax.ShapeDtypeStruct(edge, BF16),
        ],
        in_specs=[anywhere] * 5,
        out_specs=[vmem] * 5 + [anywhere] * 3,
        scratch_shapes=[
            pltpu.SMEM(occupation.shape, F32),
            pltpu.SMEM(offsets.shape, jnp.int32),
            pltpu.SMEM(neighbours.shape, jnp.int32),
            pltpu.VMEM(coupling.shape, BF16),
            pltpu.VMEM(greens.shape[1:], BF16),
            pltpu.SemaphoreType.DMA((8,)),
        ]
        + scratch(modes, slots, size, count),
        compiler_params=pltpu.CompilerParams(vmem_limit_bytes=16 << 20),
        cost_estimate=cost(shape, modes, slots),
    )(occupation, offsets, neighbours, coupling, greens)


def cost(shape, modes, slots):
    size = shape[3]
    flops = 4 * shape[1] * shape[2] * size * size * shape[4] * modes * slots
    return pl.CostEstimate(flops=flops, bytes_accessed=1 << 20, transcendentals=0)


def next_body(part, blocks, flip, wanted, n_edges, *refs):
    occ, off, nbr, rows, cols, own = refs[:6]
    edges = tuple(ref.at[0] for ref in refs[6 : 6 + n_edges])
    outs = list(refs[6 + n_edges : -2])
    outs = [outs.pop(0) if want else None for want in wanted]
    terms(part, blocks, flip, occ, off, nbr, rows, cols, own.at[0], edges, outs, refs[-2], refs[-1])


def next_call(part, blocks, flip, wanted, scalars, stacked, own, edges):
    rows, cols = stacked
    slots, wide, size = rows.shape
    modes = wide // size
    count = own[0].shape[1]
    lanes = own[3]
    shape = (1, count, len(blocks), size, lanes)
    vmem = pl.BlockSpec(memory_space=pltpu.VMEM)

    def cut(array, lead, tail, lanes):
        return pl.BlockSpec(
            (1,) + array.shape[1:-1] + (lanes,), lambda i, lead=lead, tail=tail: (lead, 0, 0, 0, tail)
        )

    def full(shape):
        return pl.BlockSpec(shape, lambda i: (0,) * len(shape))

    sources = [own] + list(edges)
    return pl.pallas_call(
        functools.partial(next_body, part, blocks, flip, wanted, len(edges)),
        out_shape=[
            jax.ShapeDtypeStruct(shape, kind) for want, kind in zip(wanted, (BF16, F32, F32)) if want
        ],
        grid=(1,),
        in_specs=[pl.BlockSpec(memory_space=pltpu.SMEM)] * 3
        + [full(rows.shape), full(cols.shape)]
        + [cut(*s) for s in sources],
        out_specs=[full(shape)] * sum(wanted),
        scratch_shapes=scratch(modes, slots, size, count),
        compiler_params=pltpu.CompilerParams(vmem_limit_bytes=16 << 20),
        cost_estimate=cost(shape, modes, slots),
    )(*scalars, rows, cols, *[s[0] for s in sources])


def add_greater(mine_in, got_in, mine_out, got_out, out):
    for mine, got, blocks in ((mine_in, got_in, (1, 2)), (mine_out, got_out, (0, 3))):
        for i, at in enumerate(blocks):
            out[0, :, at] = (mine[0, :, i] + got[0, :, i].astype(F32)).astype(BF16)


def add_lesser(mine, near, got, mine_in, got_in, mine_out, got_out, _, out):
    size = mine.shape[-1]
    out[0, :, :, :, :size] = (mine[0] + near[0] + got[0].astype(F32)).astype(BF16)
    for mine, got, blocks in ((mine_in, got_in, (1, 2)), (mine_out, got_out, (0, 3))):
        for i, at in enumerate(blocks):
            out[0, :, at, :, size:] = (mine[0, :, i] + got[0, :, i].astype(F32)).astype(BF16)


def add_up(body, part, arrays, shape, out):
    def full(shape):
        return pl.BlockSpec(shape, lambda i: (0,) * len(shape))

    given = list(arrays) + ([] if out is None else [out])
    return pl.pallas_call(
        body,
        out_shape=jax.ShapeDtypeStruct(shape, BF16),
        grid=(1,),
        in_specs=[full(a.shape) for a in arrays] + [pl.BlockSpec(memory_space=pl.ANY)] * (out is not None),
        out_specs=pl.BlockSpec((1,) + shape[1:], lambda i: (part, 0, 0, 0, 0)),
        input_output_aliases={} if out is None else {len(arrays): 0},
        compiler_params=pltpu.CompilerParams(vmem_limit_bytes=16 << 20),
        cost_estimate=pl.CostEstimate(flops=1 << 20, bytes_accessed=1 << 20, transcendentals=0),
    )(*given)


def on_device(greens, coupling, occupation, offsets, neighbours):
    slabs = lax.axis_size("slab")
    size = coupling.shape[-1]
    across = [(i, i ^ 1) for i in range(4)]
    along = [(i, i ^ 2) for i in range(4)]
    upward = [(i, i + 1) for i in range(slabs - 1)]
    downward = [(i + 1, i) for i in range(slabs - 1)]
    inner, outer, every = (1, 2), (0, 3), (0, 1, 2, 3)
    scalars = (occupation, offsets, neighbours)
    wide = 2 * size

    def relay(far):
        return lax.ppermute(far, "energy", along)

    def pass_on(near, relayed):
        return lax.ppermute((near + relayed.astype(F32)).astype(BF16), "energy", across)

    far, near_g1, mine_g1, rows, cols, raw, last, head = first_call(
        1, inner, greens, coupling, occupation, offsets, neighbours
    )
    stacked = (rows, cols)
    relay_g1 = relay(far)
    raw_x = lax.ppermute(raw, "energy", across)
    before = lax.ppermute(last, "slab", upward)
    after = lax.ppermute(head, "slab", downward)
    every_out = (True, True, True)
    far, near_l1, mine_l1 = next_call(
        0, inner, 0, every_out, scalars, stacked, (greens, 0, 1, size), ()
    )
    relay_l1 = relay(far)
    got_g1 = pass_on(near_g1, relay_g1)
    far, near_g2, mine_g2 = next_call(
        1, outer, 0, every_out, scalars, stacked, (greens, 1, 0, wide), ((before, 1, 0, wide), (after, 1, 0, wide))
    )
    relay_g2 = relay(far)
    got_l1 = pass_on(near_l1, relay_l1)
    before_x = lax.ppermute(raw_x[:, :, 3:], "slab", upward)
    after_x = lax.ppermute(raw_x[:, :, :1], "slab", downward)
    far, near_l2, mine_l2 = next_call(
        0, outer, 0, every_out, scalars, stacked, (greens, 0, 1, size), ((before, 0, 1, size), (after, 0, 1, size))
    )
    relay_l2 = relay(far)
    got_g2 = pass_on(near_g2, relay_g2)
    far, near_z = next_call(
        0, every, 1, (True, True, False), scalars, stacked, (raw_x, 0, 0, size), ((before_x, 0, 0, size), (after_x, 0, 0, size))
    )
    got_z = relay(far)
    (mine_z,) = next_call(
        0, every, 0, (False, False, True), scalars, stacked, (greens, 0, 0, size), ((before, 0, 0, size), (after, 0, 0, size))
    )
    got_l2 = pass_on(near_l2, relay_l2)
    out = add_up(add_greater, 1, (mine_g1, got_g1, mine_g2, got_g2), greens.shape, None)
    return add_up(
        add_lesser, 0, (mine_z, near_z, got_z, mine_l1, got_l1, mine_l2, got_l2), greens.shape, out
    )


def solution(mesh):
    in_specs = (P(None, "energy", "slab", None, None), P(), P(), P(), P("slab", None))
    out_specs = P(None, "energy", "slab", None, None)
    return jax.shard_map(
        on_device, mesh=mesh, in_specs=in_specs, out_specs=out_specs, check_vma=False
    )
```

```python
import functools

import jax
import jax.numpy as jnp
from jax import lax
from jax.experimental import pallas as pl
from jax.experimental.pallas import tpu as pltpu
from jax.sharding import PartitionSpec as P

BF16 = jnp.bfloat16
F32 = jnp.float32


def stack_coupling(c_ref, rows, cols):
    modes, slots, size = c_ref.shape[:3]
    for m in range(modes):
        for k in range(slots):
            c = c_ref[m, k]
            rows[k, m * size : (m + 1) * size, :] = c
            cols[m, :, k * size : (k + 1) * size] = c


def source_tile(nbr, first, owned, at, e, k, own, edges):
    listed = nbr[at, k]
    local = listed - first
    tile = own[e, jnp.clip(local, 0, owned - 1)]
    if edges:
        tile = jnp.where(local < 0, edges[0][e, 0], tile)
        tile = jnp.where(local >= owned, edges[1][e, 0], tile)
    return jnp.where(listed >= 0, tile, jnp.zeros_like(tile))


def terms(part, blocks, flip, occ, off, nbr, rows, cols, own, edges, outs, half, acc):
    far, near, mine = outs
    slots, wide, size = rows.shape
    modes = wide // size
    count, owned, _, lanes = own.shape
    per = 2 * size // lanes
    first = lax.axis_index("slab") * owned
    odd = lax.rem(lax.axis_index("energy") + flip, 2)
    step = blocks[1] - blocks[0]

    def group(i, carry):
        if per == 1:
            places = [(blocks[0] + step * i, i)]
        elif len(blocks) == 2:
            places = [(blocks[0], 0), (blocks[1], 1)]
        else:
            places = [(2 * i, 2 * i), (2 * i + 1, 2 * i + 1)]
        acc[...] = jnp.zeros_like(acc)
        for k in range(slots):
            for j in range(2):
                if per == 1:
                    src = source_tile(nbr, first, owned, places[0][0], j, k, own, edges)
                else:
                    src = jnp.concatenate(
                        [source_tile(nbr, first, owned, places[j][0], e, k, own, edges) for e in range(count)],
                        axis=1,
                    )
                r = jnp.dot(rows[k], src, preferred_element_type=F32).astype(BF16)
                for m in range(modes):
                    for h in range(2):
                        e, u = (j, h) if per == 1 else (h, j)
                        to = (e * 2 + u) * size
                        half[m, to : to + size, k * size : (k + 1) * size] = r[
                            m * size : (m + 1) * size, h * size : (h + 1) * size
                        ]

        def second(m):
            y = lax.dot_general(
                half[m], cols[m], (((1,), (1,)), ((), ())), preferred_element_type=F32
            )
            o = off[m]
            n = occ[m]
            down, up = (n + 1.0, n) if part == 0 else (n, n + 1.0)
            for e in range(count):
                for u in range(2):
                    to = (e * 2 + u) * size
                    ys = y[to : to + size]
                    acc[e - o + count, u] += down * ys
                    acc[e + o + count, u] += up * ys

        for m in range(modes):
            if far is None and near is None:
                pl.when(off[m] < count)(functools.partial(second, m))
            else:
                second(m)
        for j in range(count):
            for u in range(2):
                to, cut = (places[0][1], slice(u * size, (u + 1) * size)) if per == 1 else (places[u][1], slice(0, size))
                if far is not None:
                    far[0, j, to, :, cut] = acc[2 * count * odd + j, u].astype(BF16)
                if near is not None:
                    near[0, j, to, :, cut] = acc[2 * count * (1 - odd) + j, u]
                if mine is not None:
                    mine[0, j, to, :, cut] = acc[count + j, u]
        return carry

    groups = len(blocks) // per
    if groups == 1:
        group(0, 0)
    else:
        lax.fori_loop(0, groups, group, 0)


def scratch(modes, slots, size, count):
    return [
        pltpu.VMEM((modes, count * 2 * size, slots * size), BF16),
        pltpu.VMEM((3 * count, 2, size, size), F32),
    ]


def first_body(part, blocks, occ_h, off_h, nbr_h, c_h, g_h, far, near, mine, rows, cols, raw, last, head, occ, off, nbr, c_ref, own, sems, half, acc):
    size = c_h.shape[-1]
    owned = g_h.shape[2]
    copies = [
        pltpu.make_async_copy(src, dst, sems.at[i])
        for i, (src, dst) in enumerate(
            [
                (c_h, c_ref),
                (g_h.at[part], own),
                (occ_h, occ),
                (off_h, off),
                (nbr_h, nbr),
                (g_h.at[pl.ds(1 - part, 1), :, :, :, pl.ds(0, size)], raw),
                (g_h.at[:, :, pl.ds(owned - 1, 1)], last),
                (g_h.at[:, :, pl.ds(0, 1)], head),
            ]
        )
    ]
    for copy in copies:
        copy.start()
    copies[0].wait()
    stack_coupling(c_ref, rows, cols)
    for copy in copies[1:5]:
        copy.wait()
    terms(part, blocks, 0, occ, off, nbr, rows, cols, own, (), (far, near, mine), half, acc)
    for copy in copies[5:]:
        copy.wait()


def first_call(part, blocks, greens, coupling, occupation, offsets, neighbours):
    modes, slots, size = coupling.shape[:3]
    parts, count, owned = greens.shape[:3]
    shape = (1, count, len(blocks), size, 2 * size)
    edge = (parts, count, 1, size, 2 * size)
    anywhere = pl.BlockSpec(memory_space=pl.ANY)
    hbm = pl.BlockSpec(memory_space=pltpu.HBM)
    vmem = pl.BlockSpec(memory_space=pltpu.VMEM)
    return pl.pallas_call(
        functools.partial(first_body, part, blocks),
        out_shape=[
            jax.ShapeDtypeStruct(shape, BF16),
            jax.ShapeDtypeStruct(shape, F32),
            jax.ShapeDtypeStruct(shape, F32),
            jax.ShapeDtypeStruct((slots, modes * size, size), BF16),
            jax.ShapeDtypeStruct((modes, size, slots * size), BF16),
            jax.ShapeDtypeStruct((1, count, owned, size, size), BF16),
            jax.ShapeDtypeStruct(edge, BF16),
            jax.ShapeDtypeStruct(edge, BF16),
        ],
        in_specs=[hbm] * 5,
        out_specs=[vmem] * 5 + [anywhere] * 3,
        scratch_shapes=[
            pltpu.SMEM(occupation.shape, F32),
            pltpu.SMEM(offsets.shape, jnp.int32),
            pltpu.SMEM(neighbours.shape, jnp.int32),
            pltpu.VMEM(coupling.shape, BF16),
            pltpu.VMEM(greens.shape[1:], BF16),
            pltpu.SemaphoreType.DMA((8,)),
        ]
        + scratch(modes, slots, size, count),
        compiler_params=pltpu.CompilerParams(vmem_limit_bytes=16 << 20),
        cost_estimate=cost(shape, modes, slots),
    )(occupation, offsets, neighbours, coupling, greens)


def cost(shape, modes, slots):
    return pl.CostEstimate(flops=1024, bytes_accessed=1024, transcendentals=0)


def next_body(part, blocks, flip, wanted, n_edges, *refs):
    occ, off, nbr, rows, cols, own = refs[:6]
    edges = tuple(ref.at[0] for ref in refs[6 : 6 + n_edges])
    outs = list(refs[6 + n_edges : -2])
    outs = [outs.pop(0) if want else None for want in wanted]
    terms(part, blocks, flip, occ, off, nbr, rows, cols, own.at[0], edges, outs, refs[-2], refs[-1])


def next_call(part, blocks, flip, wanted, scalars, stacked, own, edges):
    rows, cols = stacked
    slots, wide, size = rows.shape
    modes = wide // size
    count = own[0].shape[1]
    lanes = own[3]
    shape = (1, count, len(blocks), size, lanes)
    vmem = pl.BlockSpec(memory_space=pltpu.VMEM)

    def cut(array, lead, tail, lanes):
        return pl.BlockSpec(
            (1,) + array.shape[1:-1] + (lanes,), lambda i, lead=lead, tail=tail: (lead, 0, 0, 0, tail)
        )

    def full(shape):
        return pl.BlockSpec(shape, lambda i: (0,) * len(shape))

    sources = [own] + list(edges)
    return pl.pallas_call(
        functools.partial(next_body, part, blocks, flip, wanted, len(edges)),
        out_shape=[
            jax.ShapeDtypeStruct(shape, kind) for want, kind in zip(wanted, (BF16, F32, F32)) if want
        ],
        grid=(1,),
        in_specs=[pl.BlockSpec(memory_space=pltpu.SMEM)] * 3
        + [full(rows.shape), full(cols.shape)]
        + [cut(*s) for s in sources],
        out_specs=[full(shape)] * sum(wanted),
        scratch_shapes=scratch(modes, slots, size, count),
        compiler_params=pltpu.CompilerParams(vmem_limit_bytes=16 << 20),
        cost_estimate=cost(shape, modes, slots),
    )(*scalars, rows, cols, *[s[0] for s in sources])


def add_greater(mine_in, got_in, mine_out, got_out, out):
    for mine, got, blocks in ((mine_in, got_in, (1, 2)), (mine_out, got_out, (0, 3))):
        for i, at in enumerate(blocks):
            out[0, :, at] = (mine[0, :, i] + got[0, :, i].astype(F32)).astype(BF16)


def add_lesser(mine, near, got, mine_in, got_in, mine_out, got_out, _, out):
    size = mine.shape[-1]
    out[0, :, :, :, :size] = (mine[0] + near[0] + got[0].astype(F32)).astype(BF16)
    for mine, got, blocks in ((mine_in, got_in, (1, 2)), (mine_out, got_out, (0, 3))):
        for i, at in enumerate(blocks):
            out[0, :, at, :, size:] = (mine[0, :, i] + got[0, :, i].astype(F32)).astype(BF16)


def add_up(body, part, arrays, shape, out):
    def full(shape):
        return pl.BlockSpec(shape, lambda i: (0,) * len(shape))

    given = list(arrays) + ([] if out is None else [out])
    return pl.pallas_call(
        body,
        out_shape=jax.ShapeDtypeStruct(shape, BF16),
        grid=(1,),
        in_specs=[full(a.shape) for a in arrays] + [pl.BlockSpec(memory_space=pl.ANY)] * (out is not None),
        out_specs=pl.BlockSpec((1,) + shape[1:], lambda i: (part, 0, 0, 0, 0)),
        input_output_aliases={} if out is None else {len(arrays): 0},
        compiler_params=pltpu.CompilerParams(vmem_limit_bytes=16 << 20),
        cost_estimate=pl.CostEstimate(flops=1024, bytes_accessed=1024, transcendentals=0),
    )(*given)


def on_device(greens, coupling, occupation, offsets, neighbours):
    slabs = lax.axis_size("slab")
    size = coupling.shape[-1]
    across = [(i, i ^ 1) for i in range(4)]
    along = [(i, i ^ 2) for i in range(4)]
    upward = [(i, i + 1) for i in range(slabs - 1)]
    downward = [(i + 1, i) for i in range(slabs - 1)]
    inner, outer, every = (1, 2), (0, 3), (0, 1, 2, 3)
    scalars = (occupation, offsets, neighbours)
    wide = 2 * size

    def relay(far):
        return lax.ppermute(far, "energy", along)

    def total(near, relayed):
        return (near + relayed.astype(F32)).astype(BF16)

    def pass_on(both):
        return lax.ppermute(both, "energy", across)

    def after_these(stacked, *others):
        return lax.optimization_barrier((stacked,) + others)[0]

    far, near_g1, mine_g1, rows, cols, raw, last, head = first_call(
        1, inner, greens, coupling, occupation, offsets, neighbours
    )
    stacked = (rows, cols)
    relay_g1 = relay(far)
    raw_x = lax.ppermute(raw, "energy", across)
    before = lax.ppermute(last, "slab", upward)
    after = lax.ppermute(head, "slab", downward)
    every_out = (True, True, True)
    far, near_l1, mine_l1 = next_call(
        0, inner, 0, every_out, scalars, stacked, (greens, 0, 1, size), ()
    )
    relay_l1 = relay(far)
    both_g1 = total(near_g1, relay_g1)
    got_g1 = pass_on(both_g1)
    stacked = after_these(stacked, both_g1, mine_l1)
    far, near_g2, mine_g2 = next_call(
        1, outer, 0, every_out, scalars, stacked, (greens, 1, 0, wide), ((before, 1, 0, wide), (after, 1, 0, wide))
    )
    relay_g2 = relay(far)
    last_x, head_x = after_these((raw_x[:, :, 3:], raw_x[:, :, :1]), mine_g2)
    before_x = lax.ppermute(last_x, "slab", upward)
    after_x = lax.ppermute(head_x, "slab", downward)
    stacked = after_these(stacked, last_x, head_x)
    far, near_l2, mine_l2 = next_call(
        0, outer, 0, every_out, scalars, stacked, (greens, 0, 1, size), ((before, 0, 1, size), (after, 0, 1, size))
    )
    relay_l2 = relay(far)
    both_l1 = total(near_l1, after_these(relay_l1, mine_l2))
    got_l1 = pass_on(both_l1)
    stacked = after_these(stacked, both_l1)
    far, near_z = next_call(
        0, every, 1, (True, True, False), scalars, stacked, (raw_x, 0, 0, size), ((before_x, 0, 0, size), (after_x, 0, 0, size))
    )
    got_z = relay(far)
    both_g2 = total(near_g2, after_these(relay_g2, near_z))
    got_g2 = pass_on(both_g2)
    stacked = after_these(stacked, both_g2)
    (mine_z,) = next_call(
        0, every, 0, (False, False, True), scalars, stacked, (greens, 0, 0, size), ((before, 0, 0, size), (after, 0, 0, size))
    )
    both_l2 = total(near_l2, after_these(relay_l2, mine_z))
    got_l2 = pass_on(both_l2)
    out = add_up(add_greater, 1, (mine_g1, got_g1, mine_g2, got_g2), greens.shape, None)
    return add_up(
        add_lesser, 0, (mine_z, near_z, got_z, mine_l1, got_l1, mine_l2, got_l2), greens.shape, out
    )


def solution(mesh):
    in_specs = (P(None, "energy", "slab", None, None), P(), P(), P(), P("slab", None))
    out_specs = P(None, "energy", "slab", None, None)
    return jax.shard_map(
        on_device, mesh=mesh, in_specs=in_specs, out_specs=out_specs, check_vma=False
    )
```

```python
import functools

import jax
import jax.numpy as jnp
from jax import lax
from jax.experimental import pallas as pl
from jax.experimental.pallas import tpu as pltpu
from jax.sharding import PartitionSpec as P

BF16 = jnp.bfloat16
F32 = jnp.float32

NEAR, FAR = "n", "f"
FIRST = (("full", 1, 1), ("full", 1, 2))
SECOND = (("full", 1, NEAR), ("half", 0, 1, (1, 2)))
THIRD = (("full", 1, FAR), ("half", 0, 1, (NEAR, FAR)))
RAW = (("half", 0, 0, (1, 2)), ("half", 0, 0, (NEAR, FAR)))


def stack_coupling(c_ref, rows, cols):
    modes, slots, size = c_ref.shape[:3]
    for m in range(modes):
        for k in range(slots):
            c = c_ref[m, k]
            rows[k, m * size : (m + 1) * size, :] = c
            cols[m, :, k * size : (k + 1) * size] = c


def place(block, owned):
    odd = lax.rem(lax.axis_index("slab"), 2)
    return {NEAR: (owned - 1) * (1 - odd), FAR: (owned - 1) * odd}.get(block, block)


def group_terms(group, flip, scalars, rows, cols, own, edges, outs, half, acc):
    occ, off, nbr = scalars
    far, near, mine = outs
    slots, wide, size = rows.shape
    modes = wide // size
    owned = nbr.shape[0]
    count = acc.shape[0] // 3
    first = lax.axis_index("slab") * owned
    odd = lax.rem(lax.axis_index("energy") + flip, 2)
    part = group[1]

    def source(block, k, e, lanes):
        listed = nbr[place(block, owned), k]
        local = listed - first
        tile = own(part, e, jnp.clip(local, 0, owned - 1), lanes)
        if block in (NEAR, FAR):
            outside = jnp.logical_or(local < 0, local >= owned)
            tile = jnp.where(outside, edges[block](part, e, lanes), tile)
        return jnp.where(listed >= 0, tile, jnp.zeros_like(tile))

    for k in range(slots):
        for j in range(2):
            if group[0] == "full":
                src = source(group[2], k, j, slice(0, 2 * size))
            else:
                lanes = slice(group[2] * size, (group[2] + 1) * size)
                src = jnp.concatenate([source(group[3][j], k, e, lanes) for e in range(count)], axis=1)
            r = jnp.dot(rows[k], src, preferred_element_type=F32).astype(BF16)
            for m in range(modes):
                for h in range(2):
                    e, u = (j, h) if group[0] == "full" else (h, j)
                    to = (e * 2 + u) * size
                    half[m, to : to + size, k * size : (k + 1) * size] = r[
                        m * size : (m + 1) * size, h * size : (h + 1) * size
                    ]
    acc[...] = jnp.zeros_like(acc)

    def second(m):
        y = lax.dot_general(half[m], cols[m], (((1,), (1,)), ((), ())), preferred_element_type=F32)
        o = off[m]
        n = occ[m]
        down, up = (n + 1.0, n) if part == 0 else (n, n + 1.0)
        for e in range(count):
            for u in range(2):
                to = (e * 2 + u) * size
                ys = y[to : to + size]
                acc[e - o + count, u] += down * ys
                acc[e + o + count, u] += up * ys

    for m in range(modes):
        if far is None and near is None:
            pl.when(off[m] < count)(functools.partial(second, m))
        else:
            second(m)
    if far is not None:
        far[...] = acc[pl.ds(2 * count * odd, count)].astype(BF16)
    if near is not None:
        near[...] = acc[pl.ds(2 * count * (1 - odd), count)]
    if mine is not None:
        mine[...] = acc[pl.ds(count, count)]


def pieces(size, count):
    return (2, count, 2, size, size)


def scratch(modes, slots, size, count):
    return [
        pltpu.VMEM((modes, count * 2 * size, slots * size), BF16),
        pltpu.VMEM((3 * count, 2, size, size), F32),
    ]


VMEM = pl.BlockSpec(memory_space=pltpu.VMEM)
SMEM = pl.BlockSpec(memory_space=pltpu.SMEM)
HBM = pl.BlockSpec(memory_space=pltpu.HBM)
SMALL = pl.CostEstimate(flops=1024, bytes_accessed=1024, transcendentals=0)


def first_body(occ_h, off_h, nbr_h, c_h, g_h, far_h, near_h, mine_h, rows_h, cols_h, raw_h, edge_n, edge_f, occ, off, nbr, c_ref, own, far, near, mine, rows, cols, sems, outs, half, acc):
    size = c_h.shape[-1]
    owned = g_h.shape[2]
    fetches = [
        pltpu.make_async_copy(src, dst, sems.at[i])
        for i, (src, dst) in enumerate([(c_h, c_ref), (g_h, own), (occ_h, occ), (off_h, off), (nbr_h, nbr)])
    ]
    for fetch in fetches:
        fetch.start()
    sends = []

    def send(src, dst):
        copy = pltpu.make_async_copy(src, dst, outs.at[len(sends)])
        copy.start()
        sends.append(copy)

    fetches[0].wait()
    stack_coupling(c_ref, rows, cols)
    send(rows, rows_h)
    send(cols, cols_h)
    for fetch in fetches[1:]:
        fetch.wait()
    send(own.at[0, :, :, :, pl.ds(0, size)], raw_h)
    send(own.at[:, :, place(NEAR, owned)], edge_n)
    send(own.at[:, :, place(FAR, owned)], edge_f)

    def read(part, e, at, lanes):
        return own[part, e, at, :, lanes]

    for i, group in enumerate(FIRST):
        group_terms(group, 0, (occ, off, nbr), rows, cols, read, {}, (far.at[i], near.at[i], mine.at[i]), half, acc)
        send(far.at[i], far_h.at[i])
        send(near.at[i], near_h.at[i])
        send(mine.at[i], mine_h.at[i])
    for copy in sends:
        copy.wait()


def first_call(greens, coupling, occupation, offsets, neighbours):
    modes, slots, size = coupling.shape[:3]
    parts, count, owned = greens.shape[:3]
    shape = pieces(size, count)
    rows, cols = (slots, modes * size, size), (modes, size, slots * size)
    edge = (parts, count, size, 2 * size)
    outs = [
        (shape, BF16),
        (shape, F32),
        (shape, F32),
        (rows, BF16),
        (cols, BF16),
        ((count, owned, size, size), BF16),
        (edge, BF16),
        (edge, BF16),
    ]
    return pl.pallas_call(
        first_body,
        out_shape=[jax.ShapeDtypeStruct(*out) for out in outs],
        in_specs=[HBM] * 5,
        out_specs=[HBM] * 8,
        scratch_shapes=[
            pltpu.SMEM(occupation.shape, F32),
            pltpu.SMEM(offsets.shape, jnp.int32),
            pltpu.SMEM(neighbours.shape, jnp.int32),
            pltpu.VMEM(coupling.shape, BF16),
            pltpu.VMEM(greens.shape, BF16),
        ]
        + [pltpu.VMEM(*out) for out in outs[:5]]
        + [pltpu.SemaphoreType.DMA((5,)), pltpu.SemaphoreType.DMA((11,))]
        + scratch(modes, slots, size, count),
        compiler_params=pltpu.CompilerParams(vmem_limit_bytes=58 << 20),
        cost_estimate=SMALL,
    )(occupation, offsets, neighbours, coupling, greens)


def next_body(groups, flip, wanted, with_parts, n_edges, n_copied, *refs):
    occ, off, nbr, rows, cols, own = refs[:6]
    edge_refs = dict(zip((NEAR, FAR), refs[6 : 6 + n_edges]))
    at = 6 + n_edges
    copied = refs[at : at + n_copied]
    outs = list(refs[at + n_copied : -2])
    half, acc = refs[-2:]

    def read(part, e, at, lanes):
        return own[part, e, at, :, lanes] if with_parts else own[e, at]

    def read_edge(ref, part, e, lanes):
        return ref[part, e, :, lanes] if with_parts else ref[e]

    edges = {name: functools.partial(read_edge, ref) for name, ref in edge_refs.items()}
    results = [outs.pop(0) if want else None for want in wanted]
    for array in copied:
        for block in (NEAR, FAR):
            outs.pop(0)[...] = array[:, place(block, array.shape[1])]
    for i, group in enumerate(groups):
        views = [None if ref is None else ref.at[i] for ref in results]
        group_terms(group, flip, (occ, off, nbr), rows, cols, read, edges, views, half, acc)


def next_call(groups, flip, wanted, scalars, stacked, own, edges, copied=()):
    rows, cols = stacked
    slots, wide, size = rows.shape
    count = own.shape[-4]
    shape = pieces(size, count)
    outs = [jax.ShapeDtypeStruct(shape, kind) for want, kind in zip(wanted, (BF16, F32, F32)) if want]
    outs += [jax.ShapeDtypeStruct((count, size, size), BF16)] * (2 * len(copied))
    return pl.pallas_call(
        functools.partial(next_body, groups, flip, wanted, own.ndim == 5, len(edges), len(copied)),
        out_shape=outs,
        in_specs=[SMEM] * 3 + [VMEM] * (3 + len(edges) + len(copied)),
        out_specs=[VMEM] * len(outs),
        scratch_shapes=scratch(wide // size, slots, size, count),
        compiler_params=pltpu.CompilerParams(vmem_limit_bytes=16 << 20),
        cost_estimate=SMALL,
    )(*scalars, rows, cols, own, *edges, *copied)


def early_body(mine_1, got_1, mine_2, got_2, mine_z, near_z, got_z, out, whole, edge, half, raw, sems):
    owned, size = out.shape[2], out.shape[3]
    n, f = place(NEAR, owned), place(FAR, owned)
    im, re = pl.ds(size, size), pl.ds(0, size)
    copies = []

    def send(src, dst):
        copy = pltpu.make_async_copy(src, dst, sems.at[len(copies)])
        copy.start()
        copies.append(copy)

    def tile(mine, got, g, u):
        return (mine[g, :, u] + got[g, :, u].astype(F32)).astype(BF16)

    for u in range(2):
        for g in range(2):
            whole[:, g, :, u * size : (u + 1) * size] = tile(mine_1, got_1, g, u)
        edge[:, :, u * size : (u + 1) * size] = tile(mine_2, got_2, 0, u)
        half[:, u] = tile(mine_2, got_2, 1, u)
    send(whole, out.at[1, :, pl.ds(1, 2)])
    send(edge, out.at[1, :, n])
    send(half, out.at[0, :, pl.ds(1, 2), :, im])
    for g in range(2):
        for u in range(2):
            total = mine_z[g, :, u] + near_z[g, :, u] + got_z[g, :, u].astype(F32)
            raw[:, 2 * g + u] = total.astype(BF16)
    send(raw.at[:, pl.ds(0, 2)], out.at[0, :, pl.ds(1, 2), :, re])
    send(raw.at[:, 2], out.at[0, :, n, :, re])
    send(raw.at[:, 3], out.at[0, :, f, :, re])
    for copy in copies:
        copy.wait()


def late_body(mine, got, _, out, edge, half, sems):
    owned, size = out.shape[2], out.shape[3]
    n, f = place(NEAR, owned), place(FAR, owned)
    im = pl.ds(size, size)
    for u in range(2):
        edge[:, :, u * size : (u + 1) * size] = (mine[0, :, u] + got[0, :, u].astype(F32)).astype(BF16)
        half[:, u] = (mine[1, :, u] + got[1, :, u].astype(F32)).astype(BF16)
    copies = [
        pltpu.make_async_copy(edge, out.at[1, :, f], sems.at[0]),
        pltpu.make_async_copy(half.at[:, 0], out.at[0, :, n, :, im], sems.at[1]),
        pltpu.make_async_copy(half.at[:, 1], out.at[0, :, f, :, im], sems.at[2]),
    ]
    for copy in copies:
        copy.start()
    for copy in copies:
        copy.wait()


def add_up(early, late, greens):
    count, size = greens.shape[1], greens.shape[3]
    stage = [pltpu.VMEM((count, size, 2 * size), BF16), pltpu.VMEM((count, 2, size, size), BF16)]
    out = pl.pallas_call(
        early_body,
        out_shape=jax.ShapeDtypeStruct(greens.shape, BF16),
        in_specs=[VMEM] * len(early),
        out_specs=HBM,
        scratch_shapes=[pltpu.VMEM((count, 2, size, 2 * size), BF16)]
        + stage
        + [pltpu.VMEM((count, 4, size, size), BF16), pltpu.SemaphoreType.DMA((6,))],
        compiler_params=pltpu.CompilerParams(vmem_limit_bytes=16 << 20),
        cost_estimate=SMALL,
    )(*early)
    return pl.pallas_call(
        late_body,
        out_shape=jax.ShapeDtypeStruct(greens.shape, BF16),
        in_specs=[VMEM] * len(late) + [HBM],
        out_specs=HBM,
        scratch_shapes=stage + [pltpu.SemaphoreType.DMA((3,))],
        input_output_aliases={len(late): 0},
        compiler_params=pltpu.CompilerParams(vmem_limit_bytes=16 << 20),
        cost_estimate=SMALL,
    )(*late, out)


def after_these(array, *others):
    return lax.optimization_barrier((array,) + others)[0]


def on_device(greens, coupling, occupation, offsets, neighbours):
    slabs = lax.axis_size("slab")
    scalars = (occupation, offsets, neighbours)
    chip = [(i, i ^ 1) for i in range(slabs)]
    chips = [(i, i + 1 if i % 2 else i - 1) for i in range(1, slabs - 1)]

    def across(array):
        return lax.ppermute(array, "energy", [(i, i ^ 1) for i in range(4)])

    def along(array):
        return lax.ppermute(array, "energy", [(i, i ^ 2) for i in range(4)])

    def beside(array, pairs):
        return lax.ppermute(array, "slab", pairs)

    def total(near, relayed):
        return (near + relayed.astype(F32)).astype(BF16)

    far_1, near_1, mine_1, rows, cols, raw, edge_n, edge_f = first_call(
        greens, coupling, occupation, offsets, neighbours
    )
    stacked = (rows, cols)
    relay_1 = along(far_1)
    beside_n = beside(edge_n, chip)
    raw_x = across(raw)
    beside_f = beside(edge_f, chips)
    far_2, near_2, mine_2 = next_call(SECOND, 0, (1, 1, 1), scalars, stacked, greens, (beside_n,))
    relay_2 = along(far_2)
    both_1 = total(near_1, after_these(relay_1, far_2))
    got_1 = across(both_1)
    stacked = after_these(stacked, both_1)
    far_3, near_3, mine_3, raw_n, raw_f = next_call(
        THIRD, 0, (1, 1, 1), scalars, stacked, greens, (beside_n, beside_f), (raw_x,)
    )
    relay_3 = along(far_3)
    beside_xn = beside(raw_n, chip)
    beside_xf = beside(raw_f, chips)
    both_2 = total(near_2, after_these(relay_2, near_3))
    got_2 = across(both_2)
    stacked = after_these(stacked, both_2)
    far_z, near_z = next_call(RAW, 1, (1, 1, 0), scalars, stacked, raw_x, (beside_xn, beside_xf))
    got_z = along(far_z)
    both_3 = total(near_3, after_these(relay_3, near_z))
    got_3 = across(both_3)
    stacked = after_these(stacked, both_3)
    (mine_z,) = next_call(RAW, 0, (0, 0, 1), scalars, stacked, greens, (beside_n, beside_f))
    return add_up((mine_1, got_1, mine_2, got_2, mine_z, near_z, got_z), (mine_3, got_3), greens)


def solution(mesh):
    in_specs = (P(None, "energy", "slab", None, None), P(), P(), P(), P("slab", None))
    out_specs = P(None, "energy", "slab", None, None)
    return jax.shard_map(
        on_device, mesh=mesh, in_specs=in_specs, out_specs=out_specs, check_vma=False
    )
```

```python
import functools

import jax
import jax.numpy as jnp
from jax import lax
from jax.experimental import pallas as pl
from jax.experimental.pallas import tpu as pltpu
from jax.sharding import PartitionSpec as P

BF16 = jnp.bfloat16
F32 = jnp.float32

NEAR, FAR = "n", "f"
FIRST = (("full", 1, 1), ("full", 1, 2))
SECOND = (("full", 1, NEAR), ("half", 0, 1, (1, 2)))
THIRD = (("full", 1, FAR), ("half", 0, 1, (NEAR, FAR)))
RAW = (("half", 0, 0, (1, 2)), ("half", 0, 0, (NEAR, FAR)))


def stack_coupling(c_ref, rows, cols):
    modes, slots, size = c_ref.shape[:3]
    for m in range(modes):
        for k in range(slots):
            c = c_ref[m, k]
            rows[k, m * size : (m + 1) * size, :] = c
            cols[m, :, k * size : (k + 1) * size] = c


def place(block, owned):
    odd = lax.rem(lax.axis_index("slab"), 2)
    return {NEAR: (owned - 1) * (1 - odd), FAR: (owned - 1) * odd}.get(block, block)


def group_terms(group, flip, scalars, rows, cols, own, edges, outs, half, acc):
    occ, off, nbr = scalars
    far, near, mine = outs
    slots, wide, size = rows.shape
    modes = wide // size
    owned = nbr.shape[0]
    count = acc.shape[0] // 3
    first = lax.axis_index("slab") * owned
    odd = lax.rem(lax.axis_index("energy") + flip, 2)
    part = group[1]

    def source(block, k, e, lanes):
        listed = nbr[place(block, owned), k]
        local = listed - first
        tile = own(part, e, jnp.clip(local, 0, owned - 1), lanes)
        if block in (NEAR, FAR):
            outside = jnp.logical_or(local < 0, local >= owned)
            tile = jnp.where(outside, edges[block](part, e, lanes), tile)
        return jnp.where(listed >= 0, tile, jnp.zeros_like(tile))

    for k in range(slots):
        for j in range(2):
            if group[0] == "full":
                src = source(group[2], k, j, slice(0, 2 * size))
            else:
                lanes = slice(group[2] * size, (group[2] + 1) * size)
                src = jnp.concatenate([source(group[3][j], k, e, lanes) for e in range(count)], axis=1)
            r = jnp.dot(rows[k], src, preferred_element_type=F32).astype(BF16)
            for m in range(modes):
                for h in range(2):
                    e, u = (j, h) if group[0] == "full" else (h, j)
                    to = (e * 2 + u) * size
                    half[m, to : to + size, k * size : (k + 1) * size] = r[
                        m * size : (m + 1) * size, h * size : (h + 1) * size
                    ]
    acc[...] = jnp.zeros_like(acc)

    def second(m):
        y = lax.dot_general(half[m], cols[m], (((1,), (1,)), ((), ())), preferred_element_type=F32)
        o = off[m]
        n = occ[m]
        down, up = (n + 1.0, n) if part == 0 else (n, n + 1.0)
        for e in range(count):
            for u in range(2):
                to = (e * 2 + u) * size
                ys = y[to : to + size]
                acc[e - o + count, u] += down * ys
                acc[e + o + count, u] += up * ys

    for m in range(modes):
        if far is None and near is None:
            pl.when(off[m] < count)(functools.partial(second, m))
        else:
            second(m)
    if far is not None:
        far[...] = acc[pl.ds(2 * count * odd, count)].astype(BF16)
    if near is not None:
        near[...] = acc[pl.ds(2 * count * (1 - odd), count)]
    if mine is not None:
        mine[...] = acc[pl.ds(count, count)]


def pieces(size, count):
    return (2, count, 2, size, size)


def scratch(modes, slots, size, count):
    return [
        pltpu.VMEM((modes, count * 2 * size, slots * size), BF16),
        pltpu.VMEM((3 * count, 2, size, size), F32),
    ]


VMEM = pl.BlockSpec(memory_space=pltpu.VMEM)
SMEM = pl.BlockSpec(memory_space=pltpu.SMEM)
HBM = pl.BlockSpec(memory_space=pltpu.HBM)
SMALL = pl.CostEstimate(flops=1024, bytes_accessed=1024, transcendentals=0)


def first_body(occ_h, off_h, nbr_h, c_h, g_h, far_h, near_h, mine_h, raw_h, edge_n, edge_f, occ, off, nbr, c_ref, own, far, near, mine, rows, cols, sems, outs, half, acc):
    size = c_h.shape[-1]
    owned = g_h.shape[2]
    fetches = [
        pltpu.make_async_copy(src, dst, sems.at[i])
        for i, (src, dst) in enumerate([(c_h, c_ref), (g_h, own), (occ_h, occ), (off_h, off), (nbr_h, nbr)])
    ]
    for fetch in fetches:
        fetch.start()
    sends = []

    def send(src, dst):
        copy = pltpu.make_async_copy(src, dst, outs.at[len(sends)])
        copy.start()
        sends.append(copy)

    fetches[0].wait()
    stack_coupling(c_ref, rows, cols)
    for fetch in fetches[1:]:
        fetch.wait()
    send(own.at[0, :, :, :, pl.ds(0, size)], raw_h)
    send(own.at[:, :, place(NEAR, owned)], edge_n)
    send(own.at[:, :, place(FAR, owned)], edge_f)

    def read(part, e, at, lanes):
        return own[part, e, at, :, lanes]

    for i, group in enumerate(FIRST):
        group_terms(group, 0, (occ, off, nbr), rows, cols, read, {}, (far.at[i], near.at[i], mine.at[i]), half, acc)
        send(far.at[i], far_h.at[i])
        send(near.at[i], near_h.at[i])
        send(mine.at[i], mine_h.at[i])
    for copy in sends:
        copy.wait()


def first_call(greens, coupling, occupation, offsets, neighbours):
    modes, slots, size = coupling.shape[:3]
    parts, count, owned = greens.shape[:3]
    shape = pieces(size, count)
    rows, cols = (slots, modes * size, size), (modes, size, slots * size)
    edge = (parts, count, size, 2 * size)
    outs = [
        (shape, BF16),
        (shape, F32),
        (shape, F32),
        ((count, owned, size, size), BF16),
        (edge, BF16),
        (edge, BF16),
    ]
    return pl.pallas_call(
        first_body,
        out_shape=[jax.ShapeDtypeStruct(*out) for out in outs],
        in_specs=[HBM] * 5,
        out_specs=[HBM] * 6,
        scratch_shapes=[
            pltpu.SMEM(occupation.shape, F32),
            pltpu.SMEM(offsets.shape, jnp.int32),
            pltpu.SMEM(neighbours.shape, jnp.int32),
            pltpu.VMEM(coupling.shape, BF16),
            pltpu.VMEM(greens.shape, BF16),
        ]
        + [pltpu.VMEM(*out) for out in outs[:3] + [(rows, BF16), (cols, BF16)]]
        + [pltpu.SemaphoreType.DMA((5,)), pltpu.SemaphoreType.DMA((9,))]
        + scratch(modes, slots, size, count),
        compiler_params=pltpu.CompilerParams(vmem_limit_bytes=58 << 20),
        cost_estimate=pl.CostEstimate(flops=5 << 30, bytes_accessed=16 << 20, transcendentals=0),
    )(occupation, offsets, neighbours, coupling, greens)


def next_body(groups, flip, wanted, with_parts, n_stacked, n_edges, n_copied, *refs):
    occ, off, nbr = refs[:3]
    at = 3 + n_stacked
    own = refs[at]
    edge_refs = dict(zip((NEAR, FAR), refs[at + 1 : at + 1 + n_edges]))
    at += 1 + n_edges
    copied = refs[at : at + n_copied]
    outs = list(refs[at + n_copied : -2])
    half, acc = refs[-2:]
    if n_stacked == 1:
        rows, cols = outs[-2:]
        outs = outs[:-2]
        stack_coupling(refs[3], rows, cols)
    else:
        rows, cols = refs[3:5]

    def read(part, e, at, lanes):
        return own[part, e, at, :, lanes] if with_parts else own[e, at]

    def read_edge(ref, part, e, lanes):
        return ref[part, e, :, lanes] if with_parts else ref[e]

    edges = {name: functools.partial(read_edge, ref) for name, ref in edge_refs.items()}
    results = [outs.pop(0) if want else None for want in wanted]
    for array in copied:
        for block in (NEAR, FAR):
            outs.pop(0)[...] = array[:, place(block, array.shape[1])]
    for i, group in enumerate(groups):
        views = [None if ref is None else ref.at[i] for ref in results]
        group_terms(group, flip, (occ, off, nbr), rows, cols, read, edges, views, half, acc)


def next_call(groups, flip, wanted, scalars, stacked, own, edges, copied=()):
    modes, slots, size = stacked[0].shape[:3] if len(stacked) == 1 else (stacked[1].shape[0],) + stacked[0].shape[::2]
    count = own.shape[-4]
    shape = pieces(size, count)
    outs = [jax.ShapeDtypeStruct(shape, kind) for want, kind in zip(wanted, (BF16, F32, F32)) if want]
    outs += [jax.ShapeDtypeStruct((count, size, size), BF16)] * (2 * len(copied))
    if len(stacked) == 1:
        outs.append(jax.ShapeDtypeStruct((slots, modes * size, size), BF16))
        outs.append(jax.ShapeDtypeStruct((modes, size, slots * size), BF16))
    return pl.pallas_call(
        functools.partial(next_body, groups, flip, wanted, own.ndim == 5, len(stacked), len(edges), len(copied)),
        out_shape=outs,
        in_specs=[SMEM] * 3 + [VMEM] * (1 + len(stacked) + len(edges) + len(copied)),
        out_specs=[VMEM] * len(outs),
        scratch_shapes=scratch(modes, slots, size, count),
        compiler_params=pltpu.CompilerParams(vmem_limit_bytes=16 << 20),
        cost_estimate=SMALL,
    )(*scalars, *stacked, own, *edges, *copied)


def early_body(mine_1, got_1, mine_2, got_2, mine_z, near_z, got_z, out, whole, edge, half, raw, sems):
    owned, size = out.shape[2], out.shape[3]
    n, f = place(NEAR, owned), place(FAR, owned)
    im, re = pl.ds(size, size), pl.ds(0, size)
    copies = []

    def send(src, dst):
        copy = pltpu.make_async_copy(src, dst, sems.at[len(copies)])
        copy.start()
        copies.append(copy)

    def tile(mine, got, g, u):
        return (mine[g, :, u] + got[g, :, u].astype(F32)).astype(BF16)

    for u in range(2):
        for g in range(2):
            whole[:, g, :, u * size : (u + 1) * size] = tile(mine_1, got_1, g, u)
        edge[:, :, u * size : (u + 1) * size] = tile(mine_2, got_2, 0, u)
        half[:, u] = tile(mine_2, got_2, 1, u)
    send(whole, out.at[1, :, pl.ds(1, 2)])
    send(edge, out.at[1, :, n])
    send(half, out.at[0, :, pl.ds(1, 2), :, im])
    for g in range(2):
        for u in range(2):
            total = mine_z[g, :, u] + near_z[g, :, u] + got_z[g, :, u].astype(F32)
            raw[:, 2 * g + u] = total.astype(BF16)
    send(raw.at[:, pl.ds(0, 2)], out.at[0, :, pl.ds(1, 2), :, re])
    send(raw.at[:, 2], out.at[0, :, n, :, re])
    send(raw.at[:, 3], out.at[0, :, f, :, re])
    for copy in copies:
        copy.wait()


def late_body(mine, got, _, out, edge, half, sems):
    owned, size = out.shape[2], out.shape[3]
    n, f = place(NEAR, owned), place(FAR, owned)
    im = pl.ds(size, size)
    for u in range(2):
        edge[:, :, u * size : (u + 1) * size] = (mine[0, :, u] + got[0, :, u].astype(F32)).astype(BF16)
        half[:, u] = (mine[1, :, u] + got[1, :, u].astype(F32)).astype(BF16)
    copies = [
        pltpu.make_async_copy(edge, out.at[1, :, f], sems.at[0]),
        pltpu.make_async_copy(half.at[:, 0], out.at[0, :, n, :, im], sems.at[1]),
        pltpu.make_async_copy(half.at[:, 1], out.at[0, :, f, :, im], sems.at[2]),
    ]
    for copy in copies:
        copy.start()
    for copy in copies:
        copy.wait()


def add_up(early, late, greens):
    count, size = greens.shape[1], greens.shape[3]
    stage = [pltpu.VMEM((count, size, 2 * size), BF16), pltpu.VMEM((count, 2, size, size), BF16)]
    out = pl.pallas_call(
        early_body,
        out_shape=jax.ShapeDtypeStruct(greens.shape, BF16),
        in_specs=[VMEM] * len(early),
        out_specs=HBM,
        scratch_shapes=[pltpu.VMEM((count, 2, size, 2 * size), BF16)]
        + stage
        + [pltpu.VMEM((count, 4, size, size), BF16), pltpu.SemaphoreType.DMA((6,))],
        compiler_params=pltpu.CompilerParams(vmem_limit_bytes=16 << 20),
        cost_estimate=SMALL,
    )(*early)
    return pl.pallas_call(
        late_body,
        out_shape=jax.ShapeDtypeStruct(greens.shape, BF16),
        in_specs=[VMEM] * len(late) + [HBM],
        out_specs=HBM,
        scratch_shapes=stage + [pltpu.SemaphoreType.DMA((3,))],
        input_output_aliases={len(late): 0},
        compiler_params=pltpu.CompilerParams(vmem_limit_bytes=16 << 20),
        cost_estimate=SMALL,
    )(*late, out)


def after_these(array, *others):
    return lax.optimization_barrier((array,) + others)[0]


def on_device(greens, coupling, occupation, offsets, neighbours):
    slabs = lax.axis_size("slab")
    scalars = (occupation, offsets, neighbours)
    chip = [(i, i ^ 1) for i in range(slabs)]
    chips = [(i, i + 1 if i % 2 else i - 1) for i in range(1, slabs - 1)]

    def across(array):
        return lax.ppermute(array, "energy", [(i, i ^ 1) for i in range(4)])

    def along(array):
        return lax.ppermute(array, "energy", [(i, i ^ 2) for i in range(4)])

    def beside(array, pairs):
        return lax.ppermute(array, "slab", pairs)

    def total(near, relayed):
        return (near + relayed.astype(F32)).astype(BF16)

    far_1, near_1, mine_1, raw, edge_n, edge_f = first_call(
        greens, coupling, occupation, offsets, neighbours
    )
    relay_1 = along(far_1)
    beside_n = beside(edge_n, chip)
    raw_x = across(raw)
    beside_f = beside(after_these(edge_f, beside_n), chips)
    far_2, near_2, mine_2, rows, cols = next_call(
        SECOND, 0, (1, 1, 1), scalars, (coupling,), greens, (beside_n,)
    )
    relay_2 = along(far_2)
    both_1 = total(near_1, after_these(relay_1, far_2))
    got_1 = across(both_1)
    stacked = after_these((rows, cols), both_1)
    far_3, near_3, mine_3, raw_n, raw_f = next_call(
        THIRD, 0, (1, 1, 1), scalars, stacked, greens, (beside_n, beside_f), (raw_x,)
    )
    relay_3 = along(far_3)
    beside_xn = beside(raw_n, chip)
    beside_xf = beside(raw_f, chips)
    both_2 = total(near_2, after_these(relay_2, near_3))
    got_2 = across(both_2)
    stacked = after_these(stacked, both_2, got_1)
    far_z, near_z = next_call(RAW, 1, (1, 1, 0), scalars, stacked, raw_x, (beside_xn, beside_xf))
    got_z = along(far_z)
    both_3 = total(near_3, after_these(relay_3, near_z))
    got_3 = across(both_3)
    stacked = after_these(stacked, both_3)
    (mine_z,) = next_call(RAW, 0, (0, 0, 1), scalars, stacked, greens, (beside_n, beside_f))
    return add_up((mine_1, got_1, mine_2, got_2, mine_z, near_z, got_z), (mine_3, got_3), greens)


def solution(mesh):
    in_specs = (P(None, "energy", "slab", None, None), P(), P(), P(), P("slab", None))
    out_specs = P(None, "energy", "slab", None, None)
    return jax.shard_map(
        on_device, mesh=mesh, in_specs=in_specs, out_specs=out_specs, check_vma=False
    )
```

```python
import functools

import jax
import jax.numpy as jnp
from jax import lax
from jax.experimental import pallas as pl
from jax.experimental.pallas import tpu as pltpu
from jax.sharding import PartitionSpec as P

BF16 = jnp.bfloat16
F32 = jnp.float32

NEAR, FAR = "n", "f"
FIRST = (("full", 1, 1), ("full", 1, 2))
SECOND = (("full", 1, NEAR), ("half", 0, 1, (1, 2)))
THIRD = (("full", 1, FAR), ("half", 0, 1, (NEAR, FAR)))
RAW = (("half", 0, 0, (1, 2)), ("half", 0, 0, (NEAR, FAR)))


def stack_coupling(c_ref, rows, cols):
    modes, slots, size = c_ref.shape[:3]
    for m in range(modes):
        for k in range(slots):
            c = c_ref[m, k]
            rows[k, m * size : (m + 1) * size, :] = c
            cols[m, :, k * size : (k + 1) * size] = c


def place(block, owned):
    odd = lax.rem(lax.axis_index("slab"), 2)
    return {NEAR: (owned - 1) * (1 - odd), FAR: (owned - 1) * odd}.get(block, block)


def group_terms(group, flip, scalars, rows, cols, own, edges, outs, half, acc):
    occ, off, nbr = scalars
    far, near, mine = outs
    slots, wide, size = rows.shape
    modes = wide // size
    owned = nbr.shape[0]
    count = acc.shape[0] // 3
    first = lax.axis_index("slab") * owned
    odd = lax.rem(lax.axis_index("energy") + flip, 2)
    part = group[1]

    def source(block, k, e, lanes):
        listed = nbr[place(block, owned), k]
        local = listed - first
        tile = own(part, e, jnp.clip(local, 0, owned - 1), lanes)
        if block in (NEAR, FAR):
            outside = jnp.logical_or(local < 0, local >= owned)
            tile = jnp.where(outside, edges[block](part, e, lanes), tile)
        return jnp.where(listed >= 0, tile, jnp.zeros_like(tile))

    for k in range(slots):
        for j in range(2):
            if group[0] == "full":
                src = source(group[2], k, j, slice(0, 2 * size))
            else:
                lanes = slice(group[2] * size, (group[2] + 1) * size)
                src = jnp.concatenate([source(group[3][j], k, e, lanes) for e in range(count)], axis=1)
            r = jnp.dot(rows[k], src, preferred_element_type=F32).astype(BF16)
            for m in range(modes):
                for h in range(2):
                    e, u = (j, h) if group[0] == "full" else (h, j)
                    to = (e * 2 + u) * size
                    half[m, to : to + size, k * size : (k + 1) * size] = r[
                        m * size : (m + 1) * size, h * size : (h + 1) * size
                    ]
    acc[...] = jnp.zeros_like(acc)

    def second(m):
        y = lax.dot_general(half[m], cols[m], (((1,), (1,)), ((), ())), preferred_element_type=F32)
        o = off[m]
        n = occ[m]
        down, up = (n + 1.0, n) if part == 0 else (n, n + 1.0)
        for e in range(count):
            for u in range(2):
                to = (e * 2 + u) * size
                ys = y[to : to + size]
                acc[e - o + count, u] += down * ys
                acc[e + o + count, u] += up * ys

    for m in range(modes):
        if far is None and near is None:
            pl.when(off[m] < count)(functools.partial(second, m))
        else:
            second(m)
    if far is not None:
        far[...] = acc[pl.ds(2 * count * odd, count)].astype(BF16)
    if near is not None:
        near[...] = acc[pl.ds(2 * count * (1 - odd), count)]
    if mine is not None:
        mine[...] = acc[pl.ds(count, count)]


def pieces(size, count):
    return (2, count, 2, size, size)


def scratch(modes, slots, size, count):
    return [
        pltpu.VMEM((modes, count * 2 * size, slots * size), BF16),
        pltpu.VMEM((3 * count, 2, size, size), F32),
    ]


VMEM = pl.BlockSpec(memory_space=pltpu.VMEM)
SMEM = pl.BlockSpec(memory_space=pltpu.SMEM)
HBM = pl.BlockSpec(memory_space=pltpu.HBM)
LONG = pl.CostEstimate(flops=5 << 30, bytes_accessed=16 << 20, transcendentals=0)
SMALL = pl.CostEstimate(flops=1024, bytes_accessed=1024, transcendentals=0)


def first_body(occ_h, off_h, nbr_h, c_h, g_h, far_h, near_h, mine_h, raw_h, edge_n, edge_f, occ, off, nbr, c_ref, own, far, near, mine, rows, cols, sems, outs, half, acc):
    size = c_h.shape[-1]
    owned = g_h.shape[2]
    fetches = [
        pltpu.make_async_copy(src, dst, sems.at[i])
        for i, (src, dst) in enumerate([(c_h, c_ref), (g_h, own), (occ_h, occ), (off_h, off), (nbr_h, nbr)])
    ]
    for fetch in fetches:
        fetch.start()
    sends = []

    def send(src, dst):
        copy = pltpu.make_async_copy(src, dst, outs.at[len(sends)])
        copy.start()
        sends.append(copy)

    fetches[0].wait()
    stack_coupling(c_ref, rows, cols)
    for fetch in fetches[1:]:
        fetch.wait()
    for e in range(own.shape[1]):
        send(own.at[0, e, :, :, pl.ds(0, size)], raw_h.at[:, e])
    send(own.at[:, :, place(NEAR, owned)], edge_n)
    send(own.at[:, :, place(FAR, owned)], edge_f)

    def read(part, e, at, lanes):
        return own[part, e, at, :, lanes]

    for i, group in enumerate(FIRST):
        group_terms(group, 0, (occ, off, nbr), rows, cols, read, {}, (far.at[i], near.at[i], mine.at[i]), half, acc)
        send(far.at[i], far_h.at[i])
        send(near.at[i], near_h.at[i])
        send(mine.at[i], mine_h.at[i])
    for copy in sends:
        copy.wait()


def first_call(greens, coupling, occupation, offsets, neighbours):
    modes, slots, size = coupling.shape[:3]
    parts, count, owned = greens.shape[:3]
    shape = pieces(size, count)
    rows, cols = (slots, modes * size, size), (modes, size, slots * size)
    edge = (parts, count, size, 2 * size)
    outs = [
        (shape, BF16),
        (shape, F32),
        (shape, F32),
        ((owned, count, size, size), BF16),
        (edge, BF16),
        (edge, BF16),
    ]
    return pl.pallas_call(
        first_body,
        out_shape=[jax.ShapeDtypeStruct(*out) for out in outs],
        in_specs=[HBM] * 5,
        out_specs=[HBM] * 6,
        scratch_shapes=[
            pltpu.SMEM(occupation.shape, F32),
            pltpu.SMEM(offsets.shape, jnp.int32),
            pltpu.SMEM(neighbours.shape, jnp.int32),
            pltpu.VMEM(coupling.shape, BF16),
            pltpu.VMEM(greens.shape, BF16),
        ]
        + [pltpu.VMEM(*out) for out in outs[:3] + [(rows, BF16), (cols, BF16)]]
        + [pltpu.SemaphoreType.DMA((5,)), pltpu.SemaphoreType.DMA((10,))]
        + scratch(modes, slots, size, count),
        compiler_params=pltpu.CompilerParams(vmem_limit_bytes=58 << 20),
        cost_estimate=LONG,
    )(occupation, offsets, neighbours, coupling, greens)


def next_body(groups, flip, wanted, with_parts, n_stacked, n_edges, *refs):
    occ, off, nbr = refs[:3]
    at = 3 + n_stacked
    own = refs[at]
    edge_refs = dict(zip((NEAR, FAR), refs[at + 1 : at + 1 + n_edges]))
    outs = list(refs[at + 1 + n_edges : -2])
    half, acc = refs[-2:]
    if n_stacked == 1:
        rows, cols = outs[-2:]
        outs = outs[:-2]
        stack_coupling(refs[3], rows, cols)
    else:
        rows, cols = refs[3:5]

    def read(part, e, at, lanes):
        return own[part, e, at, :, lanes] if with_parts else own[at, e]

    def read_edge(ref, part, e, lanes):
        if with_parts:
            return ref[part, e, :, lanes]
        return ref[e] if len(ref.shape) == 3 else ref[place(FAR, ref.shape[0]), e]

    edges = {name: functools.partial(read_edge, ref) for name, ref in edge_refs.items()}
    results = [outs.pop(0) if want else None for want in wanted]
    for i, group in enumerate(groups):
        views = [None if ref is None else ref.at[i] for ref in results]
        group_terms(group, flip, (occ, off, nbr), rows, cols, read, edges, views, half, acc)


def next_call(groups, flip, wanted, scalars, stacked, own, edges, estimate=None):
    modes, slots, size = stacked[0].shape[:3] if len(stacked) == 1 else (stacked[1].shape[0],) + stacked[0].shape[::2]
    count = own.shape[1]
    shape = pieces(size, count)
    outs = [jax.ShapeDtypeStruct(shape, kind) for want, kind in zip(wanted, (BF16, F32, F32)) if want]
    if len(stacked) == 1:
        outs.append(jax.ShapeDtypeStruct((slots, modes * size, size), BF16))
        outs.append(jax.ShapeDtypeStruct((modes, size, slots * size), BF16))
    return pl.pallas_call(
        functools.partial(next_body, groups, flip, wanted, own.ndim == 5, len(stacked), len(edges)),
        out_shape=outs,
        in_specs=[SMEM] * 3 + [VMEM] * (1 + len(stacked) + len(edges)),
        out_specs=[VMEM] * len(outs),
        scratch_shapes=scratch(modes, slots, size, count),
        compiler_params=pltpu.CompilerParams(vmem_limit_bytes=16 << 20),
        cost_estimate=estimate or SMALL,
    )(*scalars, *stacked, own, *edges)


def early_body(mine_1, got_1, mine_2, got_2, mine_z, near_z, got_z, out, whole, edge, half, raw, sems):
    owned, size = out.shape[2], out.shape[3]
    n, f = place(NEAR, owned), place(FAR, owned)
    im, re = pl.ds(size, size), pl.ds(0, size)
    copies = []

    def send(src, dst):
        copy = pltpu.make_async_copy(src, dst, sems.at[len(copies)])
        copy.start()
        copies.append(copy)

    def tile(mine, got, g, u):
        return (mine[g, :, u] + got[g, :, u].astype(F32)).astype(BF16)

    for u in range(2):
        for g in range(2):
            whole[:, g, :, u * size : (u + 1) * size] = tile(mine_1, got_1, g, u)
        edge[:, :, u * size : (u + 1) * size] = tile(mine_2, got_2, 0, u)
        half[:, u] = tile(mine_2, got_2, 1, u)
    send(whole, out.at[1, :, pl.ds(1, 2)])
    send(edge, out.at[1, :, n])
    send(half, out.at[0, :, pl.ds(1, 2), :, im])
    for g in range(2):
        for u in range(2):
            total = mine_z[g, :, u] + near_z[g, :, u] + got_z[g, :, u].astype(F32)
            raw[:, 2 * g + u] = total.astype(BF16)
    send(raw.at[:, pl.ds(0, 2)], out.at[0, :, pl.ds(1, 2), :, re])
    send(raw.at[:, 2], out.at[0, :, n, :, re])
    send(raw.at[:, 3], out.at[0, :, f, :, re])
    for copy in copies:
        copy.wait()


def late_body(mine, got, _, out, edge, half, sems):
    owned, size = out.shape[2], out.shape[3]
    n, f = place(NEAR, owned), place(FAR, owned)
    im = pl.ds(size, size)
    for u in range(2):
        edge[:, :, u * size : (u + 1) * size] = (mine[0, :, u] + got[0, :, u].astype(F32)).astype(BF16)
        half[:, u] = (mine[1, :, u] + got[1, :, u].astype(F32)).astype(BF16)
    copies = [
        pltpu.make_async_copy(edge, out.at[1, :, f], sems.at[0]),
        pltpu.make_async_copy(half.at[:, 0], out.at[0, :, n, :, im], sems.at[1]),
        pltpu.make_async_copy(half.at[:, 1], out.at[0, :, f, :, im], sems.at[2]),
    ]
    for copy in copies:
        copy.start()
    for copy in copies:
        copy.wait()


def add_up(early, late, greens):
    count, size = greens.shape[1], greens.shape[3]
    stage = [pltpu.VMEM((count, size, 2 * size), BF16), pltpu.VMEM((count, 2, size, size), BF16)]
    out = pl.pallas_call(
        early_body,
        out_shape=jax.ShapeDtypeStruct(greens.shape, BF16),
        in_specs=[VMEM] * len(early),
        out_specs=HBM,
        scratch_shapes=[pltpu.VMEM((count, 2, size, 2 * size), BF16)]
        + stage
        + [pltpu.VMEM((count, 4, size, size), BF16), pltpu.SemaphoreType.DMA((6,))],
        compiler_params=pltpu.CompilerParams(vmem_limit_bytes=16 << 20),
        cost_estimate=SMALL,
    )(*early)
    return pl.pallas_call(
        late_body,
        out_shape=jax.ShapeDtypeStruct(greens.shape, BF16),
        in_specs=[VMEM] * len(late) + [HBM],
        out_specs=HBM,
        scratch_shapes=stage + [pltpu.SemaphoreType.DMA((3,))],
        input_output_aliases={len(late): 0},
        compiler_params=pltpu.CompilerParams(vmem_limit_bytes=16 << 20),
        cost_estimate=SMALL,
    )(*late, out)


def after_these(array, *others):
    return lax.optimization_barrier((array,) + others)[0]


def on_device(greens, coupling, occupation, offsets, neighbours):
    slabs = lax.axis_size("slab")
    scalars = (occupation, offsets, neighbours)
    chip = [(i, i ^ 1) for i in range(slabs)]
    chips = [(i, i + 1 if i % 2 else i - 1) for i in range(1, slabs - 1)]
    odd = lax.axis_index("slab") % 2 == 1

    def across(array):
        return lax.ppermute(array, "energy", [(i, i ^ 1) for i in range(4)])

    def along(array):
        return lax.ppermute(array, "energy", [(i, i ^ 2) for i in range(4)])

    def beside(array, pairs):
        return lax.ppermute(array, "slab", pairs)

    def total(near, relayed):
        return (near + relayed.astype(F32)).astype(BF16)

    far_1, near_1, mine_1, raw, edge_n, edge_f = first_call(
        greens, coupling, occupation, offsets, neighbours
    )
    relay_1 = along(far_1)
    beside_n = beside(edge_n, chip)
    raw_x = across(raw)
    beside_f = beside(after_these(edge_f, beside_n), chips)
    far_2, near_2, mine_2, rows, cols = next_call(
        SECOND, 0, (1, 1, 1), scalars, (coupling,), greens, (beside_n,), SMALL
    )
    relay_2 = along(far_2)
    both_1 = total(near_1, after_these(relay_1, far_2))
    got_1 = across(both_1)
    stacked = after_these((rows, cols), both_1)
    far_3, near_3, mine_3 = next_call(
        THIRD, 0, (1, 1, 1), scalars, stacked, greens, (beside_n, beside_f), SMALL
    )
    relay_3 = along(far_3)
    raw_f = jnp.where(odd, raw_x[-1], raw_x[0])
    beside_xn = beside(raw_x, chip)
    beside_xf = beside(raw_f, chips)
    both_2 = total(near_2, after_these(relay_2, near_3))
    got_2 = across(both_2)
    stacked = after_these(stacked, both_2, got_1)
    far_z, near_z = next_call(RAW, 1, (1, 1, 0), scalars, stacked, raw_x, (beside_xn, beside_xf), SMALL)
    got_z = along(far_z)
    both_3 = total(near_3, after_these(relay_3, near_z))
    got_3 = across(both_3)
    stacked = after_these(stacked, both_3)
    (mine_z,) = next_call(RAW, 0, (0, 0, 1), scalars, stacked, greens, (beside_n, beside_f), SMALL)
    return add_up((mine_1, got_1, mine_2, got_2, mine_z, near_z, got_z), (mine_3, got_3), greens)


def solution(mesh):
    in_specs = (P(None, "energy", "slab", None, None), P(), P(), P(), P("slab", None))
    out_specs = P(None, "energy", "slab", None, None)
    return jax.shard_map(
        on_device, mesh=mesh, in_specs=in_specs, out_specs=out_specs, check_vma=False
    )
```

```python
import functools

import jax
import jax.numpy as jnp
from jax import lax
from jax.experimental import pallas as pl
from jax.experimental.pallas import tpu as pltpu
from jax.sharding import PartitionSpec as P

BF16 = jnp.bfloat16
F32 = jnp.float32

NEAR, FAR = "n", "f"
FIRST = (("full", 1, 1), ("full", 1, 2))
SECOND = (("full", 1, NEAR), ("half", 0, 1, (1, 2)))
THIRD = (("full", 1, FAR), ("half", 0, 1, (NEAR, FAR)))
RAW_INNER = (("half", 0, 0, (1, 2)),)
RAW_OUTER = (("half", 0, 0, (NEAR, FAR)),)


def stack_coupling(c_ref, rows, cols):
    modes, slots, size = c_ref.shape[:3]
    for m in range(modes):
        for k in range(slots):
            c = c_ref[m, k]
            rows[k, m * size : (m + 1) * size, :] = c
            cols[m, :, k * size : (k + 1) * size] = c


def place(block, owned):
    odd = lax.rem(lax.axis_index("slab"), 2)
    return {NEAR: (owned - 1) * (1 - odd), FAR: (owned - 1) * odd}.get(block, block)


def group_terms(group, flip, scalars, rows, cols, own, edges, outs, half, acc):
    occ, off, nbr = scalars
    far, near, mine = outs
    slots, wide, size = rows.shape
    modes = wide // size
    owned = nbr.shape[0]
    count = acc.shape[0] // 3
    first = lax.axis_index("slab") * owned
    odd = lax.rem(lax.axis_index("energy") + flip, 2)
    part = group[1]

    def source(block, k, e, lanes):
        listed = nbr[place(block, owned), k]
        local = listed - first
        tile = own(part, e, jnp.clip(local, 0, owned - 1), lanes)
        if block in (NEAR, FAR):
            outside = jnp.logical_or(local < 0, local >= owned)
            tile = jnp.where(outside, edges[block](part, e, lanes), tile)
        return jnp.where(listed >= 0, tile, jnp.zeros_like(tile))

    for k in range(slots):
        for j in range(2):
            if group[0] == "full":
                src = source(group[2], k, j, slice(0, 2 * size))
            else:
                lanes = slice(group[2] * size, (group[2] + 1) * size)
                src = jnp.concatenate([source(group[3][j], k, e, lanes) for e in range(count)], axis=1)
            r = jnp.dot(rows[k], src, preferred_element_type=F32).astype(BF16)
            for m in range(modes):
                for h in range(2):
                    e, u = (j, h) if group[0] == "full" else (h, j)
                    to = (e * 2 + u) * size
                    half[m, to : to + size, k * size : (k + 1) * size] = r[
                        m * size : (m + 1) * size, h * size : (h + 1) * size
                    ]
    acc[...] = jnp.zeros_like(acc)

    def second(m):
        y = lax.dot_general(half[m], cols[m], (((1,), (1,)), ((), ())), preferred_element_type=F32)
        o = off[m]
        n = occ[m]
        down, up = (n + 1.0, n) if part == 0 else (n, n + 1.0)
        for e in range(count):
            for u in range(2):
                to = (e * 2 + u) * size
                ys = y[to : to + size]
                acc[e - o + count, u] += down * ys
                acc[e + o + count, u] += up * ys

    for m in range(modes):
        if far is None and near is None:
            pl.when(off[m] < count)(functools.partial(second, m))
        else:
            second(m)
    if far is not None:
        far[...] = acc[pl.ds(2 * count * odd, count)].astype(BF16)
    if near is not None:
        near[...] = acc[pl.ds(2 * count * (1 - odd), count)]
    if mine is not None:
        mine[...] = acc[pl.ds(count, count)]


def pieces(groups, size, count):
    return (len(groups), count, 2, size, size)


def scratch(modes, slots, size, count):
    return [
        pltpu.VMEM((modes, count * 2 * size, slots * size), BF16),
        pltpu.VMEM((3 * count, 2, size, size), F32),
    ]


VMEM = pl.BlockSpec(memory_space=pltpu.VMEM)
SMEM = pl.BlockSpec(memory_space=pltpu.SMEM)
HBM = pl.BlockSpec(memory_space=pltpu.HBM)
LONG = pl.CostEstimate(flops=5 << 30, bytes_accessed=16 << 20, transcendentals=0)
MID = pl.CostEstimate(flops=5 << 29, bytes_accessed=4 << 20, transcendentals=0)
SMALL = pl.CostEstimate(flops=1024, bytes_accessed=1024, transcendentals=0)


def first_body(occ_h, off_h, nbr_h, c_h, g_h, far_h, near_h, mine_h, raw_h, edge_n, edge_f, occ, off, nbr, c_ref, own, far, near, mine, rows, cols, sems, outs, half, acc):
    size = c_h.shape[-1]
    owned = g_h.shape[2]
    fetches = [
        pltpu.make_async_copy(src, dst, sems.at[i])
        for i, (src, dst) in enumerate([(c_h, c_ref), (g_h, own), (occ_h, occ), (off_h, off), (nbr_h, nbr)])
    ]
    for fetch in fetches:
        fetch.start()
    sends = []

    def send(src, dst):
        copy = pltpu.make_async_copy(src, dst, outs.at[len(sends)])
        copy.start()
        sends.append(copy)

    fetches[0].wait()
    stack_coupling(c_ref, rows, cols)
    for fetch in fetches[1:]:
        fetch.wait()
    for e in range(own.shape[1]):
        send(own.at[0, e, :, :, pl.ds(0, size)], raw_h.at[:, e])
    send(own.at[:, :, place(NEAR, owned)], edge_n)
    send(own.at[:, :, place(FAR, owned)], edge_f)

    def read(part, e, at, lanes):
        return own[part, e, at, :, lanes]

    for i, group in enumerate(FIRST):
        group_terms(group, 0, (occ, off, nbr), rows, cols, read, {}, (far.at[i], near.at[i], mine.at[i]), half, acc)
        send(far.at[i], far_h.at[i])
        send(near.at[i], near_h.at[i])
        send(mine.at[i], mine_h.at[i])
    for copy in sends:
        copy.wait()


def first_call(greens, coupling, occupation, offsets, neighbours):
    modes, slots, size = coupling.shape[:3]
    parts, count, owned = greens.shape[:3]
    shape = pieces(FIRST, size, count)
    rows, cols = (slots, modes * size, size), (modes, size, slots * size)
    edge = (parts, count, size, 2 * size)
    outs = [
        (shape, BF16),
        (shape, F32),
        (shape, F32),
        ((owned, count, size, size), BF16),
        (edge, BF16),
        (edge, BF16),
    ]
    return pl.pallas_call(
        first_body,
        out_shape=[jax.ShapeDtypeStruct(*out) for out in outs],
        in_specs=[HBM] * 5,
        out_specs=[HBM] * 6,
        scratch_shapes=[
            pltpu.SMEM(occupation.shape, F32),
            pltpu.SMEM(offsets.shape, jnp.int32),
            pltpu.SMEM(neighbours.shape, jnp.int32),
            pltpu.VMEM(coupling.shape, BF16),
            pltpu.VMEM(greens.shape, BF16),
        ]
        + [pltpu.VMEM(*out) for out in outs[:3] + [(rows, BF16), (cols, BF16)]]
        + [pltpu.SemaphoreType.DMA((5,)), pltpu.SemaphoreType.DMA((10,))]
        + scratch(modes, slots, size, count),
        compiler_params=pltpu.CompilerParams(vmem_limit_bytes=58 << 20),
        cost_estimate=LONG,
    )(occupation, offsets, neighbours, coupling, greens)


def next_body(groups, flip, wanted, with_parts, n_stacked, n_edges, n_done, *refs):
    occ, off, nbr = refs[:3]
    at = 3 + n_stacked
    own = refs[at]
    edge_refs = dict(zip((NEAR, FAR), refs[at + 1 : at + 1 + n_edges]))
    at += 1 + n_edges
    done = refs[at : at + n_done]
    outs = list(refs[at + n_done : -2])
    half, acc = refs[-2:]
    if n_stacked == 1:
        rows, cols = outs[-2:]
        outs = outs[:-2]
        stack_coupling(refs[3], rows, cols)
    else:
        rows, cols = refs[3:5]

    def read(part, e, at, lanes):
        return own[part, e, at, :, lanes] if with_parts else own[at, e]

    def read_edge(ref, part, e, lanes):
        if with_parts:
            return ref[part, e, :, lanes]
        return ref[e] if len(ref.shape) == 3 else ref[place(FAR, ref.shape[0]), e]

    edges = {name: functools.partial(read_edge, ref) for name, ref in edge_refs.items()}
    results = [outs.pop(0) if want else None for want in wanted]
    for i, group in enumerate(groups):
        views = [None if ref is None else ref.at[i] for ref in results]
        if done:
            views[0] = results[0].at[i + 1]
        group_terms(group, flip, (occ, off, nbr), rows, cols, read, edges, views, half, acc)
    if done:
        results[0][0] = done[0][0]


def next_call(groups, flip, wanted, scalars, stacked, own, edges, estimate=None, done=()):
    modes, slots, size = stacked[0].shape[:3] if len(stacked) == 1 else (stacked[1].shape[0],) + stacked[0].shape[::2]
    count = own.shape[1]
    shape = pieces(groups, size, count)
    far = (shape[0] + len(done),) + shape[1:]
    outs = [
        jax.ShapeDtypeStruct(*out)
        for want, out in zip(wanted, ((far, BF16), (shape, F32), (shape, F32)))
        if want
    ]
    if len(stacked) == 1:
        outs.append(jax.ShapeDtypeStruct((slots, modes * size, size), BF16))
        outs.append(jax.ShapeDtypeStruct((modes, size, slots * size), BF16))
    return pl.pallas_call(
        functools.partial(next_body, groups, flip, wanted, own.ndim == 5, len(stacked), len(edges), len(done)),
        out_shape=outs,
        in_specs=[SMEM] * 3 + [VMEM] * (1 + len(stacked) + len(edges) + len(done)),
        out_specs=[VMEM] * len(outs),
        scratch_shapes=scratch(modes, slots, size, count),
        compiler_params=pltpu.CompilerParams(vmem_limit_bytes=16 << 20),
        cost_estimate=estimate or SMALL,
    )(*scalars, *stacked, own, *edges, *done)


def start_all(pairs, sems):
    copies = [pltpu.make_async_copy(src, dst, sems.at[i]) for i, (src, dst) in enumerate(pairs)]
    for copy in copies:
        copy.start()
    return copies


def early_body(mine_1, got_1, mine_2, got_2, out, whole, edge, half, sems):
    owned, size = out.shape[2], out.shape[3]
    n = place(NEAR, owned)
    im = pl.ds(size, size)

    def tile(mine, got, g, u):
        return (mine[g, :, u] + got[g, :, u].astype(F32)).astype(BF16)

    for u in range(2):
        for g in range(2):
            whole[:, g, :, u * size : (u + 1) * size] = tile(mine_1, got_1, g, u)
        edge[:, :, u * size : (u + 1) * size] = tile(mine_2, got_2, 0, u)
        half[:, u] = tile(mine_2, got_2, 1, u)
    pairs = [
        (whole, out.at[1, :, pl.ds(1, 2)]),
        (edge, out.at[1, :, n]),
        (half, out.at[0, :, pl.ds(1, 2), :, im]),
    ]
    for copy in start_all(pairs, sems):
        copy.wait()


def late_body(mine_z, *refs):
    near, (got_z, mine, got, _, out, edge, half, raw, sems) = refs[:-9], refs[-9:]
    owned, size = out.shape[2], out.shape[3]
    n, f = place(NEAR, owned), place(FAR, owned)
    re, im = pl.ds(0, size), pl.ds(size, size)
    for g in range(2):
        for u in range(2):
            part = near[g][0, :, u] if len(near) == 2 else near[0][g, :, u]
            total = mine_z[g, :, u] + part + got_z[g, :, u].astype(F32)
            raw[:, 2 * g + u] = total.astype(BF16)
    pairs = [
        (raw.at[:, pl.ds(0, 2)], out.at[0, :, pl.ds(1, 2), :, re]),
        (raw.at[:, 2], out.at[0, :, n, :, re]),
        (raw.at[:, 3], out.at[0, :, f, :, re]),
    ]
    copies = start_all(pairs, sems.at[0])
    for u in range(2):
        edge[:, :, u * size : (u + 1) * size] = (mine[0, :, u] + got[0, :, u].astype(F32)).astype(BF16)
        half[:, u] = (mine[1, :, u] + got[1, :, u].astype(F32)).astype(BF16)
    pairs = [
        (edge, out.at[1, :, f]),
        (half.at[:, 0], out.at[0, :, n, :, im]),
        (half.at[:, 1], out.at[0, :, f, :, im]),
    ]
    for copy in copies + start_all(pairs, sems.at[1]):
        copy.wait()


def add_up(early, late, greens):
    count, size = greens.shape[1], greens.shape[3]
    stage = [pltpu.VMEM((count, size, 2 * size), BF16), pltpu.VMEM((count, 2, size, size), BF16)]
    out = pl.pallas_call(
        early_body,
        out_shape=jax.ShapeDtypeStruct(greens.shape, BF16),
        in_specs=[VMEM] * len(early),
        out_specs=HBM,
        scratch_shapes=[pltpu.VMEM((count, 2, size, 2 * size), BF16)]
        + stage
        + [pltpu.SemaphoreType.DMA((3,))],
        compiler_params=pltpu.CompilerParams(vmem_limit_bytes=16 << 20),
        cost_estimate=SMALL,
    )(*early)
    return pl.pallas_call(
        late_body,
        out_shape=jax.ShapeDtypeStruct(greens.shape, BF16),
        in_specs=[VMEM] * len(late) + [HBM],
        out_specs=HBM,
        scratch_shapes=stage
        + [pltpu.VMEM((count, 4, size, size), BF16), pltpu.SemaphoreType.DMA((2, 3))],
        input_output_aliases={len(late): 0},
        compiler_params=pltpu.CompilerParams(vmem_limit_bytes=16 << 20),
        cost_estimate=SMALL,
    )(*late, out)


def after_these(array, *others):
    return lax.optimization_barrier((array,) + others)[0]


def on_device(greens, coupling, occupation, offsets, neighbours):
    slabs = lax.axis_size("slab")
    scalars = (occupation, offsets, neighbours)
    chip = [(i, i ^ 1) for i in range(slabs)]
    chips = [(i, i + 1 if i % 2 else i - 1) for i in range(1, slabs - 1)]
    odd = lax.axis_index("slab") % 2 == 1

    def across(array):
        return lax.ppermute(array, "energy", [(i, i ^ 1) for i in range(4)])

    def along(array):
        return lax.ppermute(array, "energy", [(i, i ^ 2) for i in range(4)])

    def beside(array, pairs):
        return lax.ppermute(array, "slab", pairs)

    def total(near, relayed):
        return (near + relayed.astype(F32)).astype(BF16)

    far_1, near_1, mine_1, raw, edge_n, edge_f = first_call(greens, coupling, occupation, offsets, neighbours)
    relay_1 = along(far_1)
    beside_n = beside(edge_n, chip)
    raw_x = across(raw)
    beside_f = beside(after_these(edge_f, beside_n), chips)
    far_2, near_2, mine_2, rows, cols = next_call(SECOND, 0, (1, 1, 1), scalars, (coupling,), greens, (beside_n,), SMALL)
    relay_2 = along(far_2)
    both_1 = total(near_1, after_these(relay_1, far_2))
    got_1 = across(both_1)
    stacked = (rows, cols)
    beside_xn = beside(raw_x, chip)
    stacked_3 = after_these(stacked, both_1)
    far_3, near_3, mine_3 = next_call(THIRD, 0, (1, 1, 1), scalars, stacked_3, greens, (beside_n, beside_f), MID)
    relay_3 = along(far_3)
    raw_f = jnp.where(odd, raw_x[-1], raw_x[0])
    beside_xf = beside(raw_f, chips)
    both_2 = total(near_2, after_these(relay_2, near_3))
    got_2 = across(both_2)
    far_a, near_a = next_call(RAW_INNER, 1, (1, 1, 0), scalars, after_these(stacked, both_2), raw_x, (), SMALL)
    far_b, near_b = next_call(RAW_OUTER, 1, (1, 1, 0), scalars, after_these(stacked, both_2), raw_x, (beside_xn, beside_xf), SMALL, (far_a,))
    got_z = along(far_b)
    nears = (near_a, near_b)
    both_3 = total(near_3, after_these(relay_3, near_b))
    got_3 = across(both_3)
    (mine_z,) = next_call(RAW_INNER + RAW_OUTER, 0, (0, 0, 1), scalars, stacked, greens, (beside_n, beside_f), SMALL)
    return add_up((mine_1, got_1, mine_2, got_2), (mine_z,) + nears + (got_z, mine_3, got_3), greens)


def solution(mesh):
    in_specs = (P(None, "energy", "slab", None, None), P(), P(), P(), P("slab", None))
    out_specs = P(None, "energy", "slab", None, None)
    return jax.shard_map(
        on_device, mesh=mesh, in_specs=in_specs, out_specs=out_specs, check_vma=False
    )
```

```python
import functools

import jax
import jax.numpy as jnp
from jax import lax
from jax.experimental import pallas as pl
from jax.experimental.pallas import tpu as pltpu
from jax.sharding import PartitionSpec as P

BF16 = jnp.bfloat16
F32 = jnp.float32

NEAR, FAR = "n", "f"
FIRST = (("full", 1, 1), ("full", 1, 2))
SECOND = (("full", 1, NEAR), ("half", 0, 1, (1, 2)))
THIRD = (("full", 1, FAR), ("half", 0, 1, (NEAR, FAR)))
RAW_INNER = (("half", 0, 0, (1, 2)),)
RAW_OUTER = (("half", 0, 0, (NEAR, FAR)),)


def stack_coupling(c_ref, rows, cols):
    modes, slots, size = c_ref.shape[:3]
    for m in range(modes):
        for k in range(slots):
            c = c_ref[m, k]
            rows[k, m * size : (m + 1) * size, :] = c
            cols[m, :, k * size : (k + 1) * size] = c


def place(block, owned):
    odd = lax.rem(lax.axis_index("slab"), 2)
    return {NEAR: (owned - 1) * (1 - odd), FAR: (owned - 1) * odd}.get(block, block)


def group_terms(group, flip, scalars, rows, cols, own, edges, outs, half, acc):
    occ, off, nbr = scalars
    far, near, mine = outs
    slots, wide, size = rows.shape
    modes = wide // size
    owned = nbr.shape[0]
    count = acc.shape[0] // 3
    first = lax.axis_index("slab") * owned
    odd = lax.rem(lax.axis_index("energy") + flip, 2)
    part = group[1]

    def source(block, k, e, lanes):
        listed = nbr[place(block, owned), k]
        local = listed - first
        tile = own(part, e, jnp.clip(local, 0, owned - 1), lanes)
        if block in (NEAR, FAR):
            outside = jnp.logical_or(local < 0, local >= owned)
            tile = jnp.where(outside, edges[block](part, e, lanes), tile)
        return jnp.where(listed >= 0, tile, jnp.zeros_like(tile))

    for k in range(slots):
        for j in range(2):
            if group[0] == "full":
                src = source(group[2], k, j, slice(0, 2 * size))
            else:
                lanes = slice(group[2] * size, (group[2] + 1) * size)
                src = jnp.concatenate([source(group[3][j], k, e, lanes) for e in range(count)], axis=1)
            r = jnp.dot(rows[k], src, preferred_element_type=F32).astype(BF16)
            for m in range(modes):
                for h in range(2):
                    e, u = (j, h) if group[0] == "full" else (h, j)
                    to = (e * 2 + u) * size
                    half[m, to : to + size, k * size : (k + 1) * size] = r[
                        m * size : (m + 1) * size, h * size : (h + 1) * size
                    ]
    acc[...] = jnp.zeros_like(acc)

    def second(m):
        y = lax.dot_general(half[m], cols[m], (((1,), (1,)), ((), ())), preferred_element_type=F32)
        o = off[m]
        n = occ[m]
        down, up = (n + 1.0, n) if part == 0 else (n, n + 1.0)
        for e in range(count):
            for u in range(2):
                to = (e * 2 + u) * size
                ys = y[to : to + size]
                acc[e - o + count, u] += down * ys
                acc[e + o + count, u] += up * ys

    for m in range(modes):
        if far is None and near is None:
            pl.when(off[m] < count)(functools.partial(second, m))
        else:
            second(m)
    if far is not None:
        far[...] = acc[pl.ds(2 * count * odd, count)].astype(BF16)
    if near is not None:
        near[...] = acc[pl.ds(2 * count * (1 - odd), count)]
    if mine is not None:
        mine[...] = acc[pl.ds(count, count)]


def pieces(groups, size, count):
    return (len(groups), count, 2, size, size)


def scratch(modes, slots, size, count):
    return [
        pltpu.VMEM((modes, count * 2 * size, slots * size), BF16),
        pltpu.VMEM((3 * count, 2, size, size), F32),
    ]


VMEM = pl.BlockSpec(memory_space=pltpu.VMEM)
SMEM = pl.BlockSpec(memory_space=pltpu.SMEM)
HBM = pl.BlockSpec(memory_space=pltpu.HBM)
LONG = pl.CostEstimate(flops=5 << 30, bytes_accessed=16 << 20, transcendentals=0)
MID = pl.CostEstimate(flops=5 << 29, bytes_accessed=4 << 20, transcendentals=0)
SMALL = pl.CostEstimate(flops=1024, bytes_accessed=1024, transcendentals=0)


def first_body(occ_h, off_h, nbr_h, c_h, g_h, far_h, near_h, mine_h, raw_h, edge_n, edge_f, occ, off, nbr, c_ref, own, far, near, mine, rows, cols, sems, outs, half, acc):
    size = c_h.shape[-1]
    owned = g_h.shape[2]
    fetches = [
        pltpu.make_async_copy(src, dst, sems.at[i])
        for i, (src, dst) in enumerate(
            [(c_h, c_ref), (g_h.at[1], own.at[1]), (occ_h, occ), (off_h, off), (nbr_h, nbr), (g_h.at[0], own.at[0])]
        )
    ]
    for fetch in fetches:
        fetch.start()
    sends = []

    def send(src, dst):
        copy = pltpu.make_async_copy(src, dst, outs.at[len(sends)])
        copy.start()
        sends.append(copy)

    fetches[0].wait()
    stack_coupling(c_ref, rows, cols)
    for fetch in fetches[1:5]:
        fetch.wait()

    def read(part, e, at, lanes):
        return own[part, e, at, :, lanes]

    for i, group in enumerate(FIRST):
        group_terms(group, 0, (occ, off, nbr), rows, cols, read, {}, (far.at[i], near.at[i], mine.at[i]), half, acc)
        send(far.at[i], far_h.at[i])
        send(near.at[i], near_h.at[i])
        send(mine.at[i], mine_h.at[i])
        if i == 0:
            fetches[5].wait()
            for e in range(own.shape[1]):
                send(own.at[0, e, :, :, pl.ds(0, size)], raw_h.at[:, e])
            send(own.at[:, :, place(NEAR, owned)], edge_n)
            send(own.at[:, :, place(FAR, owned)], edge_f)
    for copy in sends:
        copy.wait()


def first_call(greens, coupling, occupation, offsets, neighbours):
    modes, slots, size = coupling.shape[:3]
    parts, count, owned = greens.shape[:3]
    shape = pieces(FIRST, size, count)
    rows, cols = (slots, modes * size, size), (modes, size, slots * size)
    edge = (parts, count, size, 2 * size)
    outs = [
        (shape, BF16),
        (shape, F32),
        (shape, F32),
        ((owned, count, size, size), BF16),
        (edge, BF16),
        (edge, BF16),
    ]
    return pl.pallas_call(
        first_body,
        out_shape=[jax.ShapeDtypeStruct(*out) for out in outs],
        in_specs=[HBM] * 5,
        out_specs=[HBM] * 6,
        scratch_shapes=[
            pltpu.SMEM(occupation.shape, F32),
            pltpu.SMEM(offsets.shape, jnp.int32),
            pltpu.SMEM(neighbours.shape, jnp.int32),
            pltpu.VMEM(coupling.shape, BF16),
            pltpu.VMEM(greens.shape, BF16),
        ]
        + [pltpu.VMEM(*out) for out in outs[:3] + [(rows, BF16), (cols, BF16)]]
        + [pltpu.SemaphoreType.DMA((6,)), pltpu.SemaphoreType.DMA((10,))]
        + scratch(modes, slots, size, count),
        compiler_params=pltpu.CompilerParams(vmem_limit_bytes=58 << 20),
        cost_estimate=LONG,
    )(occupation, offsets, neighbours, coupling, greens)


def next_body(groups, flip, wanted, with_parts, n_stacked, n_edges, n_done, *refs):
    occ, off, nbr = refs[:3]
    at = 3 + n_stacked
    own = refs[at]
    edge_refs = dict(zip((NEAR, FAR), refs[at + 1 : at + 1 + n_edges]))
    at += 1 + n_edges
    done = refs[at : at + n_done]
    outs = list(refs[at + n_done : -2])
    half, acc = refs[-2:]
    if n_stacked == 1:
        rows, cols = outs[-2:]
        outs = outs[:-2]
        stack_coupling(refs[3], rows, cols)
    else:
        rows, cols = refs[3:5]

    def read(part, e, at, lanes):
        return own[part, e, at, :, lanes] if with_parts else own[at, e]

    def read_edge(ref, part, e, lanes):
        if with_parts:
            return ref[part, e, :, lanes]
        return ref[e] if len(ref.shape) == 3 else ref[place(FAR, ref.shape[0]), e]

    edges = {name: functools.partial(read_edge, ref) for name, ref in edge_refs.items()}
    results = [outs.pop(0) if want else None for want in wanted]
    for i, group in enumerate(groups):
        views = [None if ref is None else ref.at[i] for ref in results]
        if done:
            views[0] = results[0].at[i + 1]
        group_terms(group, flip, (occ, off, nbr), rows, cols, read, edges, views, half, acc)
    if done:
        results[0][0] = done[0][0]


def next_call(groups, flip, wanted, scalars, stacked, own, edges, estimate=None, done=()):
    modes, slots, size = stacked[0].shape[:3] if len(stacked) == 1 else (stacked[1].shape[0],) + stacked[0].shape[::2]
    count = own.shape[1]
    shape = pieces(groups, size, count)
    far = (shape[0] + len(done),) + shape[1:]
    outs = [
        jax.ShapeDtypeStruct(*out)
        for want, out in zip(wanted, ((far, BF16), (shape, F32), (shape, F32)))
        if want
    ]
    if len(stacked) == 1:
        outs.append(jax.ShapeDtypeStruct((slots, modes * size, size), BF16))
        outs.append(jax.ShapeDtypeStruct((modes, size, slots * size), BF16))
    return pl.pallas_call(
        functools.partial(next_body, groups, flip, wanted, own.ndim == 5, len(stacked), len(edges), len(done)),
        out_shape=outs,
        in_specs=[SMEM] * 3 + [VMEM] * (1 + len(stacked) + len(edges) + len(done)),
        out_specs=[VMEM] * len(outs),
        scratch_shapes=scratch(modes, slots, size, count),
        compiler_params=pltpu.CompilerParams(vmem_limit_bytes=16 << 20),
        cost_estimate=estimate or SMALL,
    )(*scalars, *stacked, own, *edges, *done)


def start_all(pairs, sems):
    copies = [pltpu.make_async_copy(src, dst, sems.at[i]) for i, (src, dst) in enumerate(pairs)]
    for copy in copies:
        copy.start()
    return copies


def early_body(mine_1, got_1, mine_2, got_2, mine_z, near_a, near_b, got_z, out, whole, edge, half, raw, sems):
    owned, size = out.shape[2], out.shape[3]
    n, f = place(NEAR, owned), place(FAR, owned)
    re, im = pl.ds(0, size), pl.ds(size, size)

    def tile(mine, got, g, u):
        return (mine[g, :, u] + got[g, :, u].astype(F32)).astype(BF16)

    for u in range(2):
        for g in range(2):
            whole[:, g, :, u * size : (u + 1) * size] = tile(mine_1, got_1, g, u)
        edge[:, :, u * size : (u + 1) * size] = tile(mine_2, got_2, 0, u)
        half[:, u] = tile(mine_2, got_2, 1, u)
    pairs = [
        (whole, out.at[1, :, pl.ds(1, 2)]),
        (edge, out.at[1, :, n]),
        (half, out.at[0, :, pl.ds(1, 2), :, im]),
    ]
    copies = start_all(pairs, sems.at[0])
    for g, near in enumerate((near_a, near_b)):
        for u in range(2):
            total = mine_z[g, :, u] + near[0, :, u] + got_z[g, :, u].astype(F32)
            raw[:, 2 * g + u] = total.astype(BF16)
    pairs = [
        (raw.at[:, pl.ds(0, 2)], out.at[0, :, pl.ds(1, 2), :, re]),
        (raw.at[:, 2], out.at[0, :, n, :, re]),
        (raw.at[:, 3], out.at[0, :, f, :, re]),
    ]
    for copy in copies + start_all(pairs, sems.at[1]):
        copy.wait()


def late_body(mine, got, _, out, edge, half, sems):
    owned, size = out.shape[2], out.shape[3]
    n, f = place(NEAR, owned), place(FAR, owned)
    im = pl.ds(size, size)
    for u in range(2):
        edge[:, :, u * size : (u + 1) * size] = (mine[0, :, u] + got[0, :, u].astype(F32)).astype(BF16)
        half[:, u] = (mine[1, :, u] + got[1, :, u].astype(F32)).astype(BF16)
    pairs = [
        (edge, out.at[1, :, f]),
        (half.at[:, 0], out.at[0, :, n, :, im]),
        (half.at[:, 1], out.at[0, :, f, :, im]),
    ]
    for copy in start_all(pairs, sems):
        copy.wait()


def add_up(early, late, greens):
    count, size = greens.shape[1], greens.shape[3]
    stage = [pltpu.VMEM((count, size, 2 * size), BF16), pltpu.VMEM((count, 2, size, size), BF16)]
    out = pl.pallas_call(
        early_body,
        out_shape=jax.ShapeDtypeStruct(greens.shape, BF16),
        in_specs=[VMEM] * len(early),
        out_specs=HBM,
        scratch_shapes=[pltpu.VMEM((count, 2, size, 2 * size), BF16)]
        + stage
        + [pltpu.VMEM((count, 4, size, size), BF16), pltpu.SemaphoreType.DMA((2, 3))],
        compiler_params=pltpu.CompilerParams(vmem_limit_bytes=16 << 20),
        cost_estimate=SMALL,
    )(*early)
    return pl.pallas_call(
        late_body,
        out_shape=jax.ShapeDtypeStruct(greens.shape, BF16),
        in_specs=[VMEM] * len(late) + [HBM],
        out_specs=HBM,
        scratch_shapes=stage + [pltpu.SemaphoreType.DMA((3,))],
        input_output_aliases={len(late): 0},
        compiler_params=pltpu.CompilerParams(vmem_limit_bytes=16 << 20),
        cost_estimate=SMALL,
    )(*late, out)


def total_body(near, relayed, both):
    both[...] = (near[...] + relayed[...].astype(F32)).astype(BF16)


def total_call(near, relayed):
    return pl.pallas_call(
        total_body,
        out_shape=jax.ShapeDtypeStruct(near.shape, BF16),
        in_specs=[VMEM] * 2,
        out_specs=VMEM,
        compiler_params=pltpu.CompilerParams(vmem_limit_bytes=16 << 20),
        cost_estimate=SMALL,
    )(near, relayed)


def after_these(array, *others):
    return lax.optimization_barrier((array,) + others)[0]


def on_device(greens, coupling, occupation, offsets, neighbours):
    slabs = lax.axis_size("slab")
    scalars = (occupation, offsets, neighbours)
    chip = [(i, i ^ 1) for i in range(slabs)]
    chips = [(i, i + 1 if i % 2 else i - 1) for i in range(1, slabs - 1)]

    def across(array):
        return lax.ppermute(array, "energy", [(i, i ^ 1) for i in range(4)])

    def along(array):
        return lax.ppermute(array, "energy", [(i, i ^ 2) for i in range(4)])

    def beside(array, pairs):
        return lax.ppermute(array, "slab", pairs)

    def total(near, relayed):
        return (near + relayed.astype(F32)).astype(BF16)

    far_1, near_1, mine_1, raw, edge_n, edge_f = first_call(greens, coupling, occupation, offsets, neighbours)
    relay_1 = along(far_1)
    beside_n = beside(edge_n, chip)
    raw_x = across(raw)
    beside_f = beside(after_these(edge_f, beside_n), chips)
    far_2, near_2, mine_2, rows, cols = next_call(SECOND, 0, (1, 1, 1), scalars, (coupling,), greens, (beside_n,), SMALL)
    relay_2 = along(far_2)
    both_1 = total_call(near_1, after_these(relay_1, far_2))
    got_1 = across(both_1)
    stacked = (rows, cols)
    beside_xn = beside(raw_x, chip)
    stacked_3 = after_these(stacked, both_1)
    far_3, near_3, mine_3 = next_call(THIRD, 0, (1, 1, 1), scalars, stacked_3, greens, (beside_n, beside_f), MID)
    relay_3 = along(far_3)
    size = coupling.shape[-1]
    raw_f = beside_f[0, :, :, :size]
    beside_xf = across(raw_f)
    both_2 = total_call(near_2, after_these(relay_2, near_3))
    got_2 = across(both_2)
    far_a, near_a = next_call(RAW_INNER, 1, (1, 1, 0), scalars, after_these(stacked, both_2), raw_x, (), SMALL)
    far_b, near_b = next_call(RAW_OUTER, 1, (1, 1, 0), scalars, after_these(stacked, both_2, got_1), raw_x, (beside_xn, beside_xf), SMALL, (far_a,))
    got_z = along(far_b)
    nears = (near_a, near_b)
    both_3 = total_call(near_3, after_these(relay_3, near_b))
    got_3 = across(both_3)
    (mine_z,) = next_call(RAW_INNER + RAW_OUTER, 0, (0, 0, 1), scalars, stacked, greens, (beside_n, beside_f), SMALL)
    return add_up((mine_1, got_1, mine_2, got_2, mine_z) + nears + (got_z,), (mine_3, got_3), greens)


def solution(mesh):
    in_specs = (P(None, "energy", "slab", None, None), P(), P(), P(), P("slab", None))
    out_specs = P(None, "energy", "slab", None, None)
    return jax.shard_map(
        on_device, mesh=mesh, in_specs=in_specs, out_specs=out_specs, check_vma=False
    )
```

```python
import functools

import jax
import jax.numpy as jnp
from jax import lax
from jax.experimental import pallas as pl
from jax.experimental.pallas import tpu as pltpu
from jax.sharding import PartitionSpec as P

BF16 = jnp.bfloat16
F32 = jnp.float32

NEAR, FAR = "n", "f"
FIRST = (("full", 1, 1), ("full", 1, 2))
SECOND = (("full", 1, NEAR), ("half", 0, 1, (1, 2)))
THIRD = (("full", 1, FAR), ("half", 0, 1, (NEAR, FAR)))
RAW_INNER = (("half", 0, 0, (1, 2)),)
RAW_OUTER = (("half", 0, 0, (NEAR, FAR)),)


def stack_coupling(c_ref, rows, cols):
    modes, slots, size = c_ref.shape[:3]
    for m in range(modes):
        for k in range(slots):
            c = c_ref[m, k]
            rows[k, m * size : (m + 1) * size, :] = c
            cols[m, :, k * size : (k + 1) * size] = c


def place(block, owned):
    odd = lax.rem(lax.axis_index("slab"), 2)
    return {NEAR: (owned - 1) * (1 - odd), FAR: (owned - 1) * odd}.get(block, block)


def group_terms(group, flip, scalars, rows, cols, own, edges, outs, half, acc):
    occ, off, nbr = scalars
    far, near, mine = outs
    slots, wide, size = rows.shape
    modes = wide // size
    owned = nbr.shape[0]
    count = acc.shape[0] // 3
    first = lax.axis_index("slab") * owned
    odd = lax.rem(lax.axis_index("energy") + flip, 2)
    part = group[1]

    def source(block, k, e, lanes):
        listed = nbr[place(block, owned), k]
        local = listed - first
        tile = own(part, e, jnp.clip(local, 0, owned - 1), lanes)
        if block in (NEAR, FAR):
            outside = jnp.logical_or(local < 0, local >= owned)
            tile = jnp.where(outside, edges[block](part, e, lanes), tile)
        return jnp.where(listed >= 0, tile, jnp.zeros_like(tile))

    for k in range(slots):
        for j in range(2):
            if group[0] == "full":
                src = source(group[2], k, j, slice(0, 2 * size))
            else:
                lanes = slice(group[2] * size, (group[2] + 1) * size)
                src = jnp.concatenate([source(group[3][j], k, e, lanes) for e in range(count)], axis=1)
            r = jnp.dot(rows[k], src, preferred_element_type=F32).astype(BF16)
            for m in range(modes):
                for h in range(2):
                    e, u = (j, h) if group[0] == "full" else (h, j)
                    to = (e * 2 + u) * size
                    half[m, to : to + size, k * size : (k + 1) * size] = r[
                        m * size : (m + 1) * size, h * size : (h + 1) * size
                    ]
    acc[...] = jnp.zeros_like(acc)

    def second(m):
        y = lax.dot_general(half[m], cols[m], (((1,), (1,)), ((), ())), preferred_element_type=F32)
        o = off[m]
        n = occ[m]
        down, up = (n + 1.0, n) if part == 0 else (n, n + 1.0)
        for e in range(count):
            for u in range(2):
                to = (e * 2 + u) * size
                ys = y[to : to + size]
                acc[e - o + count, u] += down * ys
                acc[e + o + count, u] += up * ys

    for m in range(modes):
        if far is None and near is None:
            pl.when(off[m] < count)(functools.partial(second, m))
        else:
            second(m)
    if far is not None:
        far[...] = acc[pl.ds(2 * count * odd, count)].astype(BF16)
    if near is not None:
        near[...] = acc[pl.ds(2 * count * (1 - odd), count)]
    if mine is not None:
        mine[...] = acc[pl.ds(count, count)]


def pieces(groups, size, count):
    return (len(groups), count, 2, size, size)


def scratch(modes, slots, size, count):
    return [
        pltpu.VMEM((modes, count * 2 * size, slots * size), BF16),
        pltpu.VMEM((3 * count, 2, size, size), F32),
    ]


VMEM = pl.BlockSpec(memory_space=pltpu.VMEM)
SMEM = pl.BlockSpec(memory_space=pltpu.SMEM)
HBM = pl.BlockSpec(memory_space=pltpu.HBM)
LONG = pl.CostEstimate(flops=5 << 30, bytes_accessed=16 << 20, transcendentals=0)
MID = pl.CostEstimate(flops=5 << 29, bytes_accessed=4 << 20, transcendentals=0)
SMALL = pl.CostEstimate(flops=1024, bytes_accessed=1024, transcendentals=0)


def first_body(occ_h, off_h, nbr_h, c_h, g_h, far_h, near_h, mine_h, raw_h, edge_n, edge_f, occ, off, nbr, c_ref, own, far, near, mine, rows, cols, sems, outs, half, acc):
    size = c_h.shape[-1]
    owned = g_h.shape[2]
    fetches = [
        pltpu.make_async_copy(src, dst, sems.at[i])
        for i, (src, dst) in enumerate(
            [(c_h, c_ref), (g_h.at[1], own.at[1]), (occ_h, occ), (off_h, off), (nbr_h, nbr), (g_h.at[0], own.at[0])]
        )
    ]
    for fetch in fetches:
        fetch.start()
    sends = []

    def send(src, dst):
        copy = pltpu.make_async_copy(src, dst, outs.at[len(sends)])
        copy.start()
        sends.append(copy)

    fetches[0].wait()
    stack_coupling(c_ref, rows, cols)
    for fetch in fetches[1:5]:
        fetch.wait()

    def read(part, e, at, lanes):
        return own[part, e, at, :, lanes]

    for i, group in enumerate(FIRST):
        group_terms(group, 0, (occ, off, nbr), rows, cols, read, {}, (far.at[i], near.at[i], mine.at[i]), half, acc)
        send(far.at[i], far_h.at[i])
        send(near.at[i], near_h.at[i])
        send(mine.at[i], mine_h.at[i])
        if i == 0:
            fetches[5].wait()
            for e in range(own.shape[1]):
                send(own.at[0, e, :, :, pl.ds(0, size)], raw_h.at[:, e])
            send(own.at[:, :, place(NEAR, owned)], edge_n)
            send(own.at[:, :, place(FAR, owned)], edge_f)
    for copy in sends:
        copy.wait()


def first_call(greens, coupling, occupation, offsets, neighbours):
    modes, slots, size = coupling.shape[:3]
    parts, count, owned = greens.shape[:3]
    shape = pieces(FIRST, size, count)
    rows, cols = (slots, modes * size, size), (modes, size, slots * size)
    edge = (parts, count, size, 2 * size)
    outs = [
        (shape, BF16),
        (shape, F32),
        (shape, F32),
        ((owned, count, size, size), BF16),
        (edge, BF16),
        (edge, BF16),
    ]
    return pl.pallas_call(
        first_body,
        out_shape=[jax.ShapeDtypeStruct(*out) for out in outs],
        in_specs=[HBM] * 5,
        out_specs=[HBM] * 6,
        scratch_shapes=[
            pltpu.SMEM(occupation.shape, F32),
            pltpu.SMEM(offsets.shape, jnp.int32),
            pltpu.SMEM(neighbours.shape, jnp.int32),
            pltpu.VMEM(coupling.shape, BF16),
            pltpu.VMEM(greens.shape, BF16),
        ]
        + [pltpu.VMEM(*out) for out in outs[:3] + [(rows, BF16), (cols, BF16)]]
        + [pltpu.SemaphoreType.DMA((6,)), pltpu.SemaphoreType.DMA((10,))]
        + scratch(modes, slots, size, count),
        compiler_params=pltpu.CompilerParams(vmem_limit_bytes=58 << 20),
        cost_estimate=LONG,
    )(occupation, offsets, neighbours, coupling, greens)


def next_body(groups, flip, wanted, with_parts, n_stacked, n_edges, n_done, *refs):
    occ, off, nbr = refs[:3]
    at = 3 + n_stacked
    own = refs[at]
    edge_refs = dict(zip((NEAR, FAR), refs[at + 1 : at + 1 + n_edges]))
    at += 1 + n_edges
    done = refs[at : at + n_done]
    outs = list(refs[at + n_done : -2])
    half, acc = refs[-2:]
    if n_stacked == 1:
        rows, cols = outs[-2:]
        outs = outs[:-2]
        stack_coupling(refs[3], rows, cols)
    else:
        rows, cols = refs[3:5]

    def read(part, e, at, lanes):
        return own[part, e, at, :, lanes] if with_parts else own[at, e]

    def read_edge(ref, part, e, lanes):
        if with_parts:
            return ref[part, e, :, lanes]
        return ref[e] if len(ref.shape) == 3 else ref[place(FAR, ref.shape[0]), e]

    edges = {name: functools.partial(read_edge, ref) for name, ref in edge_refs.items()}
    results = [outs.pop(0) if want else None for want in wanted]
    for i, group in enumerate(groups):
        views = [None if ref is None else ref.at[i] for ref in results]
        if done:
            views[0] = results[0].at[i + 1]
        group_terms(group, flip, (occ, off, nbr), rows, cols, read, edges, views, half, acc)
    if done:
        results[0][0] = done[0][0]


def next_call(groups, flip, wanted, scalars, stacked, own, edges, estimate=None, done=()):
    modes, slots, size = stacked[0].shape[:3] if len(stacked) == 1 else (stacked[1].shape[0],) + stacked[0].shape[::2]
    count = own.shape[1]
    shape = pieces(groups, size, count)
    far = (shape[0] + len(done),) + shape[1:]
    outs = [
        jax.ShapeDtypeStruct(*out)
        for want, out in zip(wanted, ((far, BF16), (shape, F32), (shape, F32)))
        if want
    ]
    if len(stacked) == 1:
        outs.append(jax.ShapeDtypeStruct((slots, modes * size, size), BF16))
        outs.append(jax.ShapeDtypeStruct((modes, size, slots * size), BF16))
    return pl.pallas_call(
        functools.partial(next_body, groups, flip, wanted, own.ndim == 5, len(stacked), len(edges), len(done)),
        out_shape=outs,
        in_specs=[SMEM] * 3 + [VMEM] * (1 + len(stacked) + len(edges) + len(done)),
        out_specs=[VMEM] * len(outs),
        scratch_shapes=scratch(modes, slots, size, count),
        compiler_params=pltpu.CompilerParams(vmem_limit_bytes=16 << 20),
        cost_estimate=estimate or SMALL,
    )(*scalars, *stacked, own, *edges, *done)


def start_all(pairs, sems):
    copies = [pltpu.make_async_copy(src, dst, sems.at[i]) for i, (src, dst) in enumerate(pairs)]
    for copy in copies:
        copy.start()
    return copies


def early_body(mine_1, got_1, mine_2, got_2, mine_z, near_a, near_b, got_z, out, whole, edge, half, raw, sems):
    owned, size = out.shape[2], out.shape[3]
    n, f = place(NEAR, owned), place(FAR, owned)
    re, im = pl.ds(0, size), pl.ds(size, size)

    def tile(mine, got, g, u):
        return (mine[g, :, u] + got[g, :, u].astype(F32)).astype(BF16)

    for u in range(2):
        for g in range(2):
            whole[:, g, :, u * size : (u + 1) * size] = tile(mine_1, got_1, g, u)
        edge[:, :, u * size : (u + 1) * size] = tile(mine_2, got_2, 0, u)
        half[:, u] = tile(mine_2, got_2, 1, u)
    pairs = [
        (whole, out.at[1, :, pl.ds(1, 2)]),
        (edge, out.at[1, :, n]),
        (half, out.at[0, :, pl.ds(1, 2), :, im]),
    ]
    copies = start_all(pairs, sems.at[0])
    for g, near in enumerate((near_a, near_b)):
        for u in range(2):
            total = mine_z[g, :, u] + near[0, :, u] + got_z[g, :, u].astype(F32)
            raw[:, 2 * g + u] = total.astype(BF16)
    pairs = [
        (raw.at[:, pl.ds(0, 2)], out.at[0, :, pl.ds(1, 2), :, re]),
        (raw.at[:, 2], out.at[0, :, n, :, re]),
        (raw.at[:, 3], out.at[0, :, f, :, re]),
    ]
    for copy in copies + start_all(pairs, sems.at[1]):
        copy.wait()


def late_body(mine, got, _, out, edge, half, sems):
    owned, size = out.shape[2], out.shape[3]
    n, f = place(NEAR, owned), place(FAR, owned)
    im = pl.ds(size, size)
    for u in range(2):
        edge[:, :, u * size : (u + 1) * size] = (mine[0, :, u] + got[0, :, u].astype(F32)).astype(BF16)
        half[:, u] = (mine[1, :, u] + got[1, :, u].astype(F32)).astype(BF16)
    pairs = [
        (edge, out.at[1, :, f]),
        (half.at[:, 0], out.at[0, :, n, :, im]),
        (half.at[:, 1], out.at[0, :, f, :, im]),
    ]
    for copy in start_all(pairs, sems):
        copy.wait()


def add_up(early, late, greens):
    count, size = greens.shape[1], greens.shape[3]
    stage = [pltpu.VMEM((count, size, 2 * size), BF16), pltpu.VMEM((count, 2, size, size), BF16)]
    out = pl.pallas_call(
        early_body,
        out_shape=jax.ShapeDtypeStruct(greens.shape, BF16),
        in_specs=[VMEM] * len(early),
        out_specs=HBM,
        scratch_shapes=[pltpu.VMEM((count, 2, size, 2 * size), BF16)]
        + stage
        + [pltpu.VMEM((count, 4, size, size), BF16), pltpu.SemaphoreType.DMA((2, 3))],
        compiler_params=pltpu.CompilerParams(vmem_limit_bytes=16 << 20),
        cost_estimate=SMALL,
    )(*early)
    return pl.pallas_call(
        late_body,
        out_shape=jax.ShapeDtypeStruct(greens.shape, BF16),
        in_specs=[VMEM] * len(late) + [HBM],
        out_specs=HBM,
        scratch_shapes=stage + [pltpu.SemaphoreType.DMA((3,))],
        input_output_aliases={len(late): 0},
        compiler_params=pltpu.CompilerParams(vmem_limit_bytes=16 << 20),
        cost_estimate=SMALL,
    )(*late, out)


def total_body(near, relayed, both):
    both[...] = (near[...] + relayed[...].astype(F32)).astype(BF16)


def total_call(near, relayed):
    return pl.pallas_call(
        total_body,
        out_shape=jax.ShapeDtypeStruct(near.shape, BF16),
        in_specs=[VMEM] * 2,
        out_specs=VMEM,
        compiler_params=pltpu.CompilerParams(vmem_limit_bytes=16 << 20),
        cost_estimate=SMALL,
    )(near, relayed)


def after_these(array, *others):
    return lax.optimization_barrier((array,) + others)[0]


def on_device(greens, coupling, occupation, offsets, neighbours):
    slabs = lax.axis_size("slab")
    scalars = (occupation, offsets, neighbours)
    chip = [(i, i ^ 1) for i in range(slabs)]
    chips = [(i, i + 1 if i % 2 else i - 1) for i in range(1, slabs - 1)]

    def across(array):
        return lax.ppermute(array, "energy", [(i, i ^ 1) for i in range(4)])

    def along(array):
        return lax.ppermute(array, "energy", [(i, i ^ 2) for i in range(4)])

    def beside(array, pairs):
        return lax.ppermute(array, "slab", pairs)

    def total(near, relayed):
        return (near + relayed.astype(F32)).astype(BF16)

    far_1, near_1, mine_1, raw, edge_n, edge_f = first_call(greens, coupling, occupation, offsets, neighbours)
    relay_1 = along(far_1)
    beside_n = beside(edge_n, chip)
    raw_x = across(after_these(raw, beside_n))
    beside_f = beside(edge_f, chips)
    far_2, near_2, mine_2, rows, cols = next_call(SECOND, 0, (1, 1, 1), scalars, (coupling,), greens, (beside_n,), SMALL)
    relay_2 = along(far_2)
    both_1 = total_call(near_1, after_these(relay_1, far_2))
    got_1 = across(both_1)
    stacked = (rows, cols)
    beside_xn = beside(raw_x, chip)
    stacked_3 = after_these(stacked, both_1)
    far_3, near_3, mine_3 = next_call(THIRD, 0, (1, 1, 1), scalars, stacked_3, greens, (beside_n, beside_f), MID)
    relay_3 = along(far_3)
    size = coupling.shape[-1]
    raw_f = beside_f[0, :, :, :size]
    beside_xf = across(raw_f)
    both_2 = total_call(near_2, after_these(relay_2, near_3))
    got_2 = across(both_2)
    far_a, near_a = next_call(RAW_INNER, 1, (1, 1, 0), scalars, after_these(stacked, both_2), raw_x, (), SMALL)
    far_b, near_b = next_call(RAW_OUTER, 1, (1, 1, 0), scalars, after_these(stacked, both_2, got_1), raw_x, (beside_xn, beside_xf), SMALL, (far_a,))
    got_z = along(far_b)
    nears = (near_a, near_b)
    both_3 = total_call(near_3, after_these(relay_3, near_b))
    got_3 = across(both_3)
    (mine_z,) = next_call(RAW_INNER + RAW_OUTER, 0, (0, 0, 1), scalars, stacked, greens, (beside_n, beside_f), SMALL)
    return add_up((mine_1, got_1, mine_2, got_2, mine_z) + nears + (got_z,), (mine_3, got_3), greens)


def solution(mesh):
    in_specs = (P(None, "energy", "slab", None, None), P(), P(), P(), P("slab", None))
    out_specs = P(None, "energy", "slab", None, None)
    return jax.shard_map(
        on_device, mesh=mesh, in_specs=in_specs, out_specs=out_specs, check_vma=False
    )
```

```python
import functools

import jax
import jax.numpy as jnp
from jax import lax
from jax.experimental import pallas as pl
from jax.experimental.pallas import tpu as pltpu
from jax.sharding import PartitionSpec as P

BF16 = jnp.bfloat16
F32 = jnp.float32

NEAR, FAR = "n", "f"
ROWS = 32
FIRST = (("full", 1, 1), ("full", 1, 2))
SECOND = (("full", 1, NEAR), ("half", 0, 1, (1, 2)))
THIRD = (("full", 1, FAR), ("half", 0, 1, (NEAR, FAR)))
RAW_INNER = (("half", 0, 0, (1, 2)),)
RAW_OUTER = (("half", 0, 0, (NEAR, FAR)),)


def stack_coupling(c_ref, rows, cols):
    modes, slots, size = c_ref.shape[:3]
    for m in range(modes):
        for k in range(slots):
            c = c_ref[m, k]
            rows[k, m * size : (m + 1) * size, :] = c
            cols[m, :, k * size : (k + 1) * size] = c


def place(block, owned):
    odd = lax.rem(lax.axis_index("slab"), 2)
    return {NEAR: (owned - 1) * (1 - odd), FAR: (owned - 1) * odd}.get(block, block)


def group_terms(group, flip, scalars, rows, cols, own, edges, outs, half, acc):
    occ, off, nbr = scalars
    far, near, mine = outs
    slots, wide, size = rows.shape
    modes = wide // size
    owned = nbr.shape[0]
    count = acc.shape[1] // (2 * size)
    first = lax.axis_index("slab") * owned
    odd = lax.rem(lax.axis_index("energy") + flip, 2)
    part = group[1]

    def source(block, k, e, lanes):
        listed = nbr[place(block, owned), k]
        local = listed - first
        tile = own(part, e, jnp.clip(local, 0, owned - 1), lanes)
        if block in (NEAR, FAR):
            outside = jnp.logical_or(local < 0, local >= owned)
            tile = jnp.where(outside, edges[block](part, e, lanes), tile)
        return jnp.where(listed >= 0, tile, jnp.zeros_like(tile))

    for k in range(slots):
        for j in range(2):
            if group[0] == "full":
                src = source(group[2], k, j, slice(0, 2 * size))
            else:
                lanes = slice(group[2] * size, (group[2] + 1) * size)
                src = jnp.concatenate([source(group[3][j], k, e, lanes) for e in range(count)], axis=1)
            r = jnp.dot(rows[k], src, preferred_element_type=F32).astype(BF16)
            for m in range(modes):
                for h in range(2):
                    e, u = (j, h) if group[0] == "full" else (h, j)
                    to = (e * 2 + u) * size
                    half[m, to : to + size, k * size : (k + 1) * size] = r[
                        m * size : (m + 1) * size, h * size : (h + 1) * size
                    ]
    for m in range(modes):
        acc[m] = lax.dot_general(half[m], cols[m], (((1,), (1,)), ((), ())), preferred_element_type=F32)
    weights = []
    for m in range(modes):
        n = occ[m]
        down, up = (n + 1.0, n) if part == 0 else (n, n + 1.0)
        one = off[m] == 1
        weights.append(
            {
                -1: jnp.where(one, down, 0.0),
                1: jnp.where(one, up, 0.0),
                -2: jnp.where(one, 0.0, down),
                2: jnp.where(one, 0.0, up),
            }
        )
    is_odd = odd == 1
    for u in range(2):
        for r in range(0, size, ROWS):
            y = [
                [acc[m, (e * 2 + u) * size + r : (e * 2 + u) * size + r + ROWS] for m in range(modes)]
                for e in range(count)
            ]

            def shifted(e, by):
                return sum(weights[m][by] * y[e][m] for m in range(modes))

            to = slice(r, r + ROWS)
            if far is not None:
                before = (shifted(0, -2), shifted(0, -1) + shifted(1, -2))
                after = (shifted(0, 2) + shifted(1, 1), shifted(1, 2))
                for j in range(count):
                    far[j, u, to] = jnp.where(is_odd, after[j], before[j]).astype(BF16)
                    near[j, u, to] = jnp.where(is_odd, before[j], after[j])
            if mine is not None:
                mine[0, u, to] = shifted(1, -1)
                mine[1, u, to] = shifted(0, 1)


def pieces(groups, size, count):
    return (len(groups), count, 2, size, size)


def scratch(modes, slots, size, count):
    return [
        pltpu.VMEM((modes, count * 2 * size, slots * size), BF16),
        pltpu.VMEM((modes, count * 2 * size, size), F32),
    ]


VMEM = pl.BlockSpec(memory_space=pltpu.VMEM)
SMEM = pl.BlockSpec(memory_space=pltpu.SMEM)
HBM = pl.BlockSpec(memory_space=pltpu.HBM)
LONG = pl.CostEstimate(flops=5 << 30, bytes_accessed=16 << 20, transcendentals=0)
MID = pl.CostEstimate(flops=5 << 29, bytes_accessed=4 << 20, transcendentals=0)
SMALL = pl.CostEstimate(flops=1024, bytes_accessed=1024, transcendentals=0)


def first_body(occ_h, off_h, nbr_h, c_h, g_h, far_h, near_h, mine_h, raw_h, edge_n, edge_f, occ, off, nbr, c_ref, own, far, near, mine, rows, cols, sems, outs, half, acc):
    size = c_h.shape[-1]
    owned = g_h.shape[2]
    fetches = [
        pltpu.make_async_copy(src, dst, sems.at[i])
        for i, (src, dst) in enumerate(
            [(c_h, c_ref), (g_h.at[1], own.at[1]), (occ_h, occ), (off_h, off), (nbr_h, nbr), (g_h.at[0], own.at[0])]
        )
    ]
    for fetch in fetches:
        fetch.start()
    sends = []

    def send(src, dst):
        copy = pltpu.make_async_copy(src, dst, outs.at[len(sends)])
        copy.start()
        sends.append(copy)

    fetches[0].wait()
    stack_coupling(c_ref, rows, cols)
    for fetch in fetches[1:5]:
        fetch.wait()

    def read(part, e, at, lanes):
        return own[part, e, at, :, lanes]

    for i, group in enumerate(FIRST):
        group_terms(group, 0, (occ, off, nbr), rows, cols, read, {}, (far.at[i], near.at[i], mine.at[i]), half, acc)
        send(far.at[i], far_h.at[i])
        send(near.at[i], near_h.at[i])
        send(mine.at[i], mine_h.at[i])
        if i == 0:
            fetches[5].wait()
            for e in range(own.shape[1]):
                send(own.at[0, e, :, :, pl.ds(0, size)], raw_h.at[:, e])
            send(own.at[:, :, place(NEAR, owned)], edge_n)
            send(own.at[:, :, place(FAR, owned)], edge_f)
    for copy in sends:
        copy.wait()


def first_call(greens, coupling, occupation, offsets, neighbours):
    modes, slots, size = coupling.shape[:3]
    parts, count, owned = greens.shape[:3]
    shape = pieces(FIRST, size, count)
    rows, cols = (slots, modes * size, size), (modes, size, slots * size)
    edge = (parts, count, size, 2 * size)
    outs = [
        (shape, BF16),
        (shape, F32),
        (shape, F32),
        ((owned, count, size, size), BF16),
        (edge, BF16),
        (edge, BF16),
    ]
    return pl.pallas_call(
        first_body,
        out_shape=[jax.ShapeDtypeStruct(*out) for out in outs],
        in_specs=[HBM] * 5,
        out_specs=[HBM] * 6,
        scratch_shapes=[
            pltpu.SMEM(occupation.shape, F32),
            pltpu.SMEM(offsets.shape, jnp.int32),
            pltpu.SMEM(neighbours.shape, jnp.int32),
            pltpu.VMEM(coupling.shape, BF16),
            pltpu.VMEM(greens.shape, BF16),
        ]
        + [pltpu.VMEM(*out) for out in outs[:3] + [(rows, BF16), (cols, BF16)]]
        + [pltpu.SemaphoreType.DMA((6,)), pltpu.SemaphoreType.DMA((10,))]
        + scratch(modes, slots, size, count),
        compiler_params=pltpu.CompilerParams(vmem_limit_bytes=58 << 20),
        cost_estimate=LONG,
    )(occupation, offsets, neighbours, coupling, greens)


def next_body(groups, flip, wanted, with_parts, n_stacked, n_edges, n_done, *refs):
    occ, off, nbr = refs[:3]
    at = 3 + n_stacked
    own = refs[at]
    edge_refs = dict(zip((NEAR, FAR), refs[at + 1 : at + 1 + n_edges]))
    at += 1 + n_edges
    done = refs[at : at + n_done]
    outs = list(refs[at + n_done : -2])
    half, acc = refs[-2:]
    if n_stacked == 1:
        rows, cols = outs[-2:]
        outs = outs[:-2]
        stack_coupling(refs[3], rows, cols)
    else:
        rows, cols = refs[3:5]

    def read(part, e, at, lanes):
        return own[part, e, at, :, lanes] if with_parts else own[at, e]

    def read_edge(ref, part, e, lanes):
        if with_parts:
            return ref[part, e, :, lanes]
        return ref[e] if len(ref.shape) == 3 else ref[place(FAR, ref.shape[0]), e]

    edges = {name: functools.partial(read_edge, ref) for name, ref in edge_refs.items()}
    results = [outs.pop(0) if want else None for want in wanted]
    for i, group in enumerate(groups):
        views = [None if ref is None else ref.at[i] for ref in results]
        if done:
            views[0] = results[0].at[i + 1]
        group_terms(group, flip, (occ, off, nbr), rows, cols, read, edges, views, half, acc)
    if done:
        results[0][0] = done[0][0]


def next_call(groups, flip, wanted, scalars, stacked, own, edges, estimate=None, done=()):
    modes, slots, size = stacked[0].shape[:3] if len(stacked) == 1 else (stacked[1].shape[0],) + stacked[0].shape[::2]
    count = own.shape[1]
    shape = pieces(groups, size, count)
    far = (shape[0] + len(done),) + shape[1:]
    outs = [
        jax.ShapeDtypeStruct(*out)
        for want, out in zip(wanted, ((far, BF16), (shape, F32), (shape, F32)))
        if want
    ]
    if len(stacked) == 1:
        outs.append(jax.ShapeDtypeStruct((slots, modes * size, size), BF16))
        outs.append(jax.ShapeDtypeStruct((modes, size, slots * size), BF16))
    return pl.pallas_call(
        functools.partial(next_body, groups, flip, wanted, own.ndim == 5, len(stacked), len(edges), len(done)),
        out_shape=outs,
        in_specs=[SMEM] * 3 + [VMEM] * (1 + len(stacked) + len(edges) + len(done)),
        out_specs=[VMEM] * len(outs),
        scratch_shapes=scratch(modes, slots, size, count),
        compiler_params=pltpu.CompilerParams(vmem_limit_bytes=16 << 20),
        cost_estimate=estimate or SMALL,
    )(*scalars, *stacked, own, *edges, *done)


def start_all(pairs, sems):
    copies = [pltpu.make_async_copy(src, dst, sems.at[i]) for i, (src, dst) in enumerate(pairs)]
    for copy in copies:
        copy.start()
    return copies


def early_body(mine_1, got_1, mine_2, got_2, mine_z, near_a, near_b, got_z, out, whole, edge, half, raw, sems):
    owned, size = out.shape[2], out.shape[3]
    n, f = place(NEAR, owned), place(FAR, owned)
    re, im = pl.ds(0, size), pl.ds(size, size)

    def tile(mine, got, g, u):
        return (mine[g, :, u] + got[g, :, u].astype(F32)).astype(BF16)

    for u in range(2):
        for g in range(2):
            whole[:, g, :, u * size : (u + 1) * size] = tile(mine_1, got_1, g, u)
        edge[:, :, u * size : (u + 1) * size] = tile(mine_2, got_2, 0, u)
        half[:, u] = tile(mine_2, got_2, 1, u)
    pairs = [
        (whole, out.at[1, :, pl.ds(1, 2)]),
        (edge, out.at[1, :, n]),
        (half, out.at[0, :, pl.ds(1, 2), :, im]),
    ]
    copies = start_all(pairs, sems.at[0])
    for g, near in enumerate((near_a, near_b)):
        for u in range(2):
            total = mine_z[g, :, u] + near[0, :, u] + got_z[g, :, u].astype(F32)
            raw[:, 2 * g + u] = total.astype(BF16)
    pairs = [
        (raw.at[:, pl.ds(0, 2)], out.at[0, :, pl.ds(1, 2), :, re]),
        (raw.at[:, 2], out.at[0, :, n, :, re]),
        (raw.at[:, 3], out.at[0, :, f, :, re]),
    ]
    for copy in copies + start_all(pairs, sems.at[1]):
        copy.wait()


def late_body(mine, got, _, out, edge, half, sems):
    owned, size = out.shape[2], out.shape[3]
    n, f = place(NEAR, owned), place(FAR, owned)
    im = pl.ds(size, size)
    for u in range(2):
        edge[:, :, u * size : (u + 1) * size] = (mine[0, :, u] + got[0, :, u].astype(F32)).astype(BF16)
        half[:, u] = (mine[1, :, u] + got[1, :, u].astype(F32)).astype(BF16)
    pairs = [
        (edge, out.at[1, :, f]),
        (half.at[:, 0], out.at[0, :, n, :, im]),
        (half.at[:, 1], out.at[0, :, f, :, im]),
    ]
    for copy in start_all(pairs, sems):
        copy.wait()


def add_up(early, late, greens):
    count, size = greens.shape[1], greens.shape[3]
    stage = [pltpu.VMEM((count, size, 2 * size), BF16), pltpu.VMEM((count, 2, size, size), BF16)]
    out = pl.pallas_call(
        early_body,
        out_shape=jax.ShapeDtypeStruct(greens.shape, BF16),
        in_specs=[VMEM] * len(early),
        out_specs=HBM,
        scratch_shapes=[pltpu.VMEM((count, 2, size, 2 * size), BF16)]
        + stage
        + [pltpu.VMEM((count, 4, size, size), BF16), pltpu.SemaphoreType.DMA((2, 3))],
        compiler_params=pltpu.CompilerParams(vmem_limit_bytes=16 << 20),
        cost_estimate=SMALL,
    )(*early)
    return pl.pallas_call(
        late_body,
        out_shape=jax.ShapeDtypeStruct(greens.shape, BF16),
        in_specs=[VMEM] * len(late) + [HBM],
        out_specs=HBM,
        scratch_shapes=stage + [pltpu.SemaphoreType.DMA((3,))],
        input_output_aliases={len(late): 0},
        compiler_params=pltpu.CompilerParams(vmem_limit_bytes=16 << 20),
        cost_estimate=SMALL,
    )(*late, out)


def total_body(near, relayed, both):
    both[...] = (near[...] + relayed[...].astype(F32)).astype(BF16)


def total_call(near, relayed):
    return pl.pallas_call(
        total_body,
        out_shape=jax.ShapeDtypeStruct(near.shape, BF16),
        in_specs=[VMEM] * 2,
        out_specs=VMEM,
        compiler_params=pltpu.CompilerParams(vmem_limit_bytes=16 << 20),
        cost_estimate=SMALL,
    )(near, relayed)


def after_these(array, *others):
    return lax.optimization_barrier((array,) + others)[0]


def on_device(greens, coupling, occupation, offsets, neighbours):
    slabs = lax.axis_size("slab")
    scalars = (occupation, offsets, neighbours)
    chip = [(i, i ^ 1) for i in range(slabs)]
    chips = [(i, i + 1 if i % 2 else i - 1) for i in range(1, slabs - 1)]

    def across(array):
        return lax.ppermute(array, "energy", [(i, i ^ 1) for i in range(4)])

    def along(array):
        return lax.ppermute(array, "energy", [(i, i ^ 2) for i in range(4)])

    def beside(array, pairs):
        return lax.ppermute(array, "slab", pairs)

    def total(near, relayed):
        return (near + relayed.astype(F32)).astype(BF16)

    far_1, near_1, mine_1, raw, edge_n, edge_f = first_call(greens, coupling, occupation, offsets, neighbours)
    relay_1 = along(far_1)
    beside_n = beside(edge_n, chip)
    raw_x = across(after_these(raw, beside_n))
    beside_f = beside(edge_f, chips)
    far_2, near_2, mine_2, rows, cols = next_call(SECOND, 0, (1, 1, 1), scalars, (coupling,), greens, (beside_n,), SMALL)
    relay_2 = along(far_2)
    both_1 = total_call(near_1, after_these(relay_1, far_2))
    got_1 = across(both_1)
    stacked = (rows, cols)
    beside_xn = beside(raw_x, chip)
    stacked_3 = after_these(stacked, both_1)
    far_3, near_3, mine_3 = next_call(THIRD, 0, (1, 1, 1), scalars, stacked_3, greens, (beside_n, beside_f), MID)
    relay_3 = along(far_3)
    size = coupling.shape[-1]
    raw_f = beside_f[0, :, :, :size]
    beside_xf = across(raw_f)
    both_2 = total_call(near_2, after_these(relay_2, near_3))
    got_2 = across(both_2)
    far_a, near_a = next_call(RAW_INNER, 1, (1, 1, 0), scalars, after_these(stacked, both_2), raw_x, (), SMALL)
    far_b, near_b = next_call(RAW_OUTER, 1, (1, 1, 0), scalars, after_these(stacked, both_2, got_1), raw_x, (beside_xn, beside_xf), SMALL, (far_a,))
    got_z = along(far_b)
    nears = (near_a, near_b)
    both_3 = total_call(near_3, after_these(relay_3, near_b))
    got_3 = across(both_3)
    (mine_z,) = next_call(RAW_INNER + RAW_OUTER, 0, (0, 0, 1), scalars, stacked, greens, (beside_n, beside_f), SMALL)
    return add_up((mine_1, got_1, mine_2, got_2, mine_z) + nears + (got_z,), (mine_3, got_3), greens)


def solution(mesh):
    in_specs = (P(None, "energy", "slab", None, None), P(), P(), P(), P("slab", None))
    out_specs = P(None, "energy", "slab", None, None)
    return jax.shard_map(
        on_device, mesh=mesh, in_specs=in_specs, out_specs=out_specs, check_vma=False
    )
```

```python
import functools

import jax
import jax.numpy as jnp
from jax import lax
from jax.experimental import pallas as pl
from jax.experimental.pallas import tpu as pltpu
from jax.sharding import PartitionSpec as P

BF16 = jnp.bfloat16
F32 = jnp.float32

NEAR, FAR = "n", "f"
ROWS = 32
FIRST = (("full", 1, 1), ("full", 1, 2))
SECOND = (("full", 1, NEAR), ("half", 0, 1, (1, 2)))
THIRD = (("full", 1, FAR), ("half", 0, 1, (NEAR, FAR)))
RAW_INNER = (("half", 0, 0, (1, 2)),)
RAW_OUTER = (("half", 0, 0, (NEAR, FAR)),)


def stack_coupling(c_ref, rows, cols):
    modes, slots, size = c_ref.shape[:3]
    for m in range(modes):
        for k in range(slots):
            c = c_ref[m, k]
            rows[k, m * size : (m + 1) * size, :] = c
            cols[m, :, k * size : (k + 1) * size] = c


def place(block, owned):
    odd = lax.rem(lax.axis_index("slab"), 2)
    return {NEAR: (owned - 1) * (1 - odd), FAR: (owned - 1) * odd}.get(block, block)


def group_terms(group, flip, scalars, rows, cols, own, edges, outs, half, acc):
    occ, off, nbr = scalars
    far, near, mine = outs
    slots, wide, size = rows.shape
    modes = wide // size
    owned = nbr.shape[0]
    count = acc.shape[1] // (2 * size)
    first = lax.axis_index("slab") * owned
    odd = lax.rem(lax.axis_index("energy") + flip, 2)
    part = group[1]

    def source(block, k, e, lanes):
        listed = nbr[place(block, owned), k]
        local = listed - first
        tile = own(part, e, jnp.clip(local, 0, owned - 1), lanes)
        if block in (NEAR, FAR):
            outside = jnp.logical_or(local < 0, local >= owned)
            tile = jnp.where(outside, edges[block](part, e, lanes), tile)
        return jnp.where(listed >= 0, tile, jnp.zeros_like(tile))

    for k in range(slots):
        for j in range(2):
            if group[0] == "full":
                src = source(group[2], k, j, slice(0, 2 * size))
            else:
                lanes = slice(group[2] * size, (group[2] + 1) * size)
                src = jnp.concatenate([source(group[3][j], k, e, lanes) for e in range(count)], axis=1)
            r = jnp.dot(rows[k], src, preferred_element_type=F32).astype(BF16)
            for m in range(modes):
                for h in range(2):
                    e, u = (j, h) if group[0] == "full" else (h, j)
                    to = (e * 2 + u) * size
                    half[m, to : to + size, k * size : (k + 1) * size] = r[
                        m * size : (m + 1) * size, h * size : (h + 1) * size
                    ]
    for m in range(modes):
        acc[m] = lax.dot_general(half[m], cols[m], (((1,), (1,)), ((), ())), preferred_element_type=F32)
    weights = []
    for m in range(modes):
        n = occ[m]
        down, up = (n + 1.0, n) if part == 0 else (n, n + 1.0)
        one = off[m] == 1
        weights.append(
            {
                -1: jnp.where(one, down, 0.0),
                1: jnp.where(one, up, 0.0),
                -2: jnp.where(one, 0.0, down),
                2: jnp.where(one, 0.0, up),
            }
        )
    is_odd = odd == 1
    for u in range(2):
        for r in range(0, size, ROWS):
            y = [
                [acc[m, (e * 2 + u) * size + r : (e * 2 + u) * size + r + ROWS] for m in range(modes)]
                for e in range(count)
            ]

            def shifted(e, by):
                return sum(weights[m][by] * y[e][m] for m in range(modes))

            to = slice(r, r + ROWS)
            if far is not None:
                before = (shifted(0, -2), shifted(0, -1) + shifted(1, -2))
                after = (shifted(0, 2) + shifted(1, 1), shifted(1, 2))
                for j in range(count):
                    far[j, u, to] = jnp.where(is_odd, after[j], before[j]).astype(BF16)
                    near[j, u, to] = jnp.where(is_odd, before[j], after[j])
            if mine is not None:
                mine[0, u, to] = shifted(1, -1)
                mine[1, u, to] = shifted(0, 1)


def pieces(groups, size, count):
    return (len(groups), count, 2, size, size)


def scratch(modes, slots, size, count):
    return [
        pltpu.VMEM((modes, count * 2 * size, slots * size), BF16),
        pltpu.VMEM((modes, count * 2 * size, size), F32),
    ]


VMEM = pl.BlockSpec(memory_space=pltpu.VMEM)
SMEM = pl.BlockSpec(memory_space=pltpu.SMEM)
HBM = pl.BlockSpec(memory_space=pltpu.HBM)
LONG = pl.CostEstimate(flops=5 << 30, bytes_accessed=16 << 20, transcendentals=0)
MID = pl.CostEstimate(flops=5 << 29, bytes_accessed=4 << 20, transcendentals=0)
SMALL = pl.CostEstimate(flops=1024, bytes_accessed=1024, transcendentals=0)


def first_body(occ_h, off_h, nbr_h, c_h, g_h, far_h, near_h, mine_h, raw_h, edge_n, edge_f, occ, off, nbr, c_ref, own, far, near, mine, rows, cols, sems, outs, half, acc):
    size = c_h.shape[-1]
    owned = g_h.shape[2]
    fetches = [
        pltpu.make_async_copy(src, dst, sems.at[i])
        for i, (src, dst) in enumerate(
            [(c_h, c_ref), (g_h.at[1], own.at[1]), (occ_h, occ), (off_h, off), (nbr_h, nbr), (g_h.at[0], own.at[0])]
        )
    ]
    for fetch in fetches:
        fetch.start()
    sends = []

    def send(src, dst):
        copy = pltpu.make_async_copy(src, dst, outs.at[len(sends)])
        copy.start()
        sends.append(copy)

    fetches[0].wait()
    stack_coupling(c_ref, rows, cols)
    for fetch in fetches[1:5]:
        fetch.wait()

    def read(part, e, at, lanes):
        return own[part, e, at, :, lanes]

    for i, group in enumerate(FIRST):
        group_terms(group, 0, (occ, off, nbr), rows, cols, read, {}, (far.at[i], near.at[i], mine.at[i]), half, acc)
        send(far.at[i], far_h.at[i])
        send(near.at[i], near_h.at[i])
        send(mine.at[i], mine_h.at[i])
        if i == 0:
            fetches[5].wait()
            for e in range(own.shape[1]):
                send(own.at[0, e, :, :, pl.ds(0, size)], raw_h.at[:, e])
            send(own.at[:, :, place(NEAR, owned)], edge_n)
            send(own.at[:, :, place(FAR, owned)], edge_f)
    for copy in sends:
        copy.wait()


def first_call(greens, coupling, occupation, offsets, neighbours):
    modes, slots, size = coupling.shape[:3]
    parts, count, owned = greens.shape[:3]
    shape = pieces(FIRST, size, count)
    rows, cols = (slots, modes * size, size), (modes, size, slots * size)
    edge = (parts, count, size, 2 * size)
    outs = [
        (shape, BF16),
        (shape, F32),
        (shape, F32),
        ((owned, count, size, size), BF16),
        (edge, BF16),
        (edge, BF16),
    ]
    return pl.pallas_call(
        first_body,
        out_shape=[jax.ShapeDtypeStruct(*out) for out in outs],
        in_specs=[HBM] * 5,
        out_specs=[HBM] * 6,
        scratch_shapes=[
            pltpu.SMEM(occupation.shape, F32),
            pltpu.SMEM(offsets.shape, jnp.int32),
            pltpu.SMEM(neighbours.shape, jnp.int32),
            pltpu.VMEM(coupling.shape, BF16),
            pltpu.VMEM(greens.shape, BF16),
        ]
        + [pltpu.VMEM(*out) for out in outs[:3] + [(rows, BF16), (cols, BF16)]]
        + [pltpu.SemaphoreType.DMA((6,)), pltpu.SemaphoreType.DMA((10,))]
        + scratch(modes, slots, size, count),
        compiler_params=pltpu.CompilerParams(vmem_limit_bytes=58 << 20),
        cost_estimate=LONG,
    )(occupation, offsets, neighbours, coupling, greens)


def next_body(groups, flip, wanted, with_parts, n_stacked, n_edges, n_done, *refs):
    occ, off, nbr = refs[:3]
    at = 3 + n_stacked
    own = refs[at]
    edge_refs = dict(zip((NEAR, FAR), refs[at + 1 : at + 1 + n_edges]))
    at += 1 + n_edges
    done = refs[at : at + n_done]
    outs = list(refs[at + n_done : -2])
    half, acc = refs[-2:]
    if n_stacked == 1:
        rows, cols = outs[-2:]
        outs = outs[:-2]
        stack_coupling(refs[3], rows, cols)
    else:
        rows, cols = refs[3:5]

    def read(part, e, at, lanes):
        return own[part, e, at, :, lanes] if with_parts else own[at, e]

    def read_edge(ref, part, e, lanes):
        if with_parts:
            return ref[part, e, :, lanes]
        return ref[e] if len(ref.shape) == 3 else ref[place(FAR, ref.shape[0]), e]

    edges = {name: functools.partial(read_edge, ref) for name, ref in edge_refs.items()}
    results = [outs.pop(0) if want else None for want in wanted]
    for i, group in enumerate(groups):
        views = [None if ref is None else ref.at[i] for ref in results]
        if done:
            views[0] = results[0].at[i + 1]
        group_terms(group, flip, (occ, off, nbr), rows, cols, read, edges, views, half, acc)
    if done:
        results[0][0] = done[0][0]


def next_call(groups, flip, wanted, scalars, stacked, own, edges, estimate=None, done=()):
    modes, slots, size = stacked[0].shape[:3] if len(stacked) == 1 else (stacked[1].shape[0],) + stacked[0].shape[::2]
    count = own.shape[1]
    shape = pieces(groups, size, count)
    far = (shape[0] + len(done),) + shape[1:]
    outs = [
        jax.ShapeDtypeStruct(*out)
        for want, out in zip(wanted, ((far, BF16), (shape, F32), (shape, F32)))
        if want
    ]
    if len(stacked) == 1:
        outs.append(jax.ShapeDtypeStruct((slots, modes * size, size), BF16))
        outs.append(jax.ShapeDtypeStruct((modes, size, slots * size), BF16))
    return pl.pallas_call(
        functools.partial(next_body, groups, flip, wanted, own.ndim == 5, len(stacked), len(edges), len(done)),
        out_shape=outs,
        in_specs=[SMEM] * 3 + [VMEM] * (1 + len(stacked) + len(edges) + len(done)),
        out_specs=[VMEM] * len(outs),
        scratch_shapes=scratch(modes, slots, size, count),
        compiler_params=pltpu.CompilerParams(vmem_limit_bytes=16 << 20),
        cost_estimate=estimate or SMALL,
    )(*scalars, *stacked, own, *edges, *done)


def start_all(pairs, sems):
    copies = [pltpu.make_async_copy(src, dst, sems.at[i]) for i, (src, dst) in enumerate(pairs)]
    for copy in copies:
        copy.start()
    return copies


def early_body(mine_1, got_1, mine_2, got_2, mine_z, near_a, near_b, got_z, out, whole, edge, half, raw, sems):
    owned, size = out.shape[2], out.shape[3]
    n, f = place(NEAR, owned), place(FAR, owned)
    re, im = pl.ds(0, size), pl.ds(size, size)

    def tile(mine, got, g, u):
        return (mine[g, :, u] + got[g, :, u].astype(F32)).astype(BF16)

    for u in range(2):
        for g in range(2):
            whole[:, g, :, u * size : (u + 1) * size] = tile(mine_1, got_1, g, u)
        edge[:, :, u * size : (u + 1) * size] = tile(mine_2, got_2, 0, u)
        half[:, u] = tile(mine_2, got_2, 1, u)
    pairs = [
        (whole, out.at[1, :, pl.ds(1, 2)]),
        (edge, out.at[1, :, n]),
        (half, out.at[0, :, pl.ds(1, 2), :, im]),
    ]
    copies = start_all(pairs, sems.at[0])
    for g, near in enumerate((near_a, near_b)):
        for u in range(2):
            total = mine_z[g, :, u] + near[0, :, u] + got_z[g, :, u].astype(F32)
            raw[:, 2 * g + u] = total.astype(BF16)
    pairs = [
        (raw.at[:, pl.ds(0, 2)], out.at[0, :, pl.ds(1, 2), :, re]),
        (raw.at[:, 2], out.at[0, :, n, :, re]),
        (raw.at[:, 3], out.at[0, :, f, :, re]),
    ]
    for copy in copies + start_all(pairs, sems.at[1]):
        copy.wait()


def late_body(mine, got, _, out, edge, half, sems):
    owned, size = out.shape[2], out.shape[3]
    n, f = place(NEAR, owned), place(FAR, owned)
    im = pl.ds(size, size)
    for u in range(2):
        edge[:, :, u * size : (u + 1) * size] = (mine[0, :, u] + got[0, :, u].astype(F32)).astype(BF16)
        half[:, u] = (mine[1, :, u] + got[1, :, u].astype(F32)).astype(BF16)
    pairs = [
        (edge, out.at[1, :, f]),
        (half.at[:, 0], out.at[0, :, n, :, im]),
        (half.at[:, 1], out.at[0, :, f, :, im]),
    ]
    for copy in start_all(pairs, sems):
        copy.wait()


def add_up(early, late, greens):
    count, size = greens.shape[1], greens.shape[3]
    stage = [pltpu.VMEM((count, size, 2 * size), BF16), pltpu.VMEM((count, 2, size, size), BF16)]
    out = pl.pallas_call(
        early_body,
        out_shape=jax.ShapeDtypeStruct(greens.shape, BF16),
        in_specs=[VMEM] * len(early),
        out_specs=HBM,
        scratch_shapes=[pltpu.VMEM((count, 2, size, 2 * size), BF16)]
        + stage
        + [pltpu.VMEM((count, 4, size, size), BF16), pltpu.SemaphoreType.DMA((2, 3))],
        compiler_params=pltpu.CompilerParams(vmem_limit_bytes=16 << 20),
        cost_estimate=SMALL,
    )(*early)
    return pl.pallas_call(
        late_body,
        out_shape=jax.ShapeDtypeStruct(greens.shape, BF16),
        in_specs=[VMEM] * len(late) + [HBM],
        out_specs=HBM,
        scratch_shapes=stage + [pltpu.SemaphoreType.DMA((3,))],
        input_output_aliases={len(late): 0},
        compiler_params=pltpu.CompilerParams(vmem_limit_bytes=16 << 20),
        cost_estimate=SMALL,
    )(*late, out)


def total_body(near, relayed, both):
    both[...] = (near[...] + relayed[...].astype(F32)).astype(BF16)


def total_call(near, relayed):
    return pl.pallas_call(
        total_body,
        out_shape=jax.ShapeDtypeStruct(near.shape, BF16),
        in_specs=[VMEM] * 2,
        out_specs=VMEM,
        compiler_params=pltpu.CompilerParams(vmem_limit_bytes=16 << 20),
        cost_estimate=SMALL,
    )(near, relayed)


def after_these(array, *others):
    return lax.optimization_barrier((array,) + others)[0]


def on_device(greens, coupling, occupation, offsets, neighbours):
    slabs = lax.axis_size("slab")
    scalars = (occupation, offsets, neighbours)
    chip = [(i, i ^ 1) for i in range(slabs)]
    chips = [(i, i + 1 if i % 2 else i - 1) for i in range(1, slabs - 1)]

    def across(array):
        return lax.ppermute(array, "energy", [(i, i ^ 1) for i in range(4)])

    def along(array):
        return lax.ppermute(array, "energy", [(i, i ^ 2) for i in range(4)])

    def beside(array, pairs):
        return lax.ppermute(array, "slab", pairs)

    def total(near, relayed):
        return (near + relayed.astype(F32)).astype(BF16)

    far_1, near_1, mine_1, raw, edge_n, edge_f = first_call(greens, coupling, occupation, offsets, neighbours)
    relay_1 = along(far_1)
    beside_n = beside(edge_n, chip)
    raw_x = across(after_these(raw, beside_n))
    beside_f = beside(edge_f, chips)
    far_2, near_2, mine_2, rows, cols = next_call(SECOND, 0, (1, 1, 1), scalars, (coupling,), greens, (beside_n,), SMALL)
    relay_2 = along(far_2)
    both_1 = total_call(near_1, after_these(relay_1, far_2))
    got_1 = across(both_1)
    stacked = (rows, cols)
    beside_xn = beside(raw_x, chip)
    stacked_3 = after_these(stacked, both_1)
    far_3, near_3, mine_3 = next_call(THIRD, 0, (1, 1, 1), scalars, stacked_3, greens, (beside_n, beside_f), SMALL)
    relay_3 = along(far_3)
    size = coupling.shape[-1]
    raw_f = beside_f[0, :, :, :size]
    beside_xf = across(raw_f)
    both_2 = total_call(near_2, after_these(relay_2, near_3))
    got_2 = across(both_2)
    far_a, near_a = next_call(RAW_INNER, 1, (1, 1, 0), scalars, after_these(stacked, both_2), raw_x, (), SMALL)
    far_b, near_b = next_call(RAW_OUTER, 1, (1, 1, 0), scalars, after_these(stacked, both_2, got_1), raw_x, (beside_xn, beside_xf), SMALL, (far_a,))
    got_z = along(far_b)
    nears = (near_a, near_b)
    both_3 = total_call(near_3, after_these(relay_3, near_b))
    got_3 = across(both_3)
    (mine_z,) = next_call(RAW_INNER + RAW_OUTER, 0, (0, 0, 1), scalars, stacked, greens, (beside_n, beside_f), SMALL)
    return add_up((mine_1, got_1, mine_2, got_2, mine_z) + nears + (got_z,), (mine_3, got_3), greens)


def solution(mesh):
    in_specs = (P(None, "energy", "slab", None, None), P(), P(), P(), P("slab", None))
    out_specs = P(None, "energy", "slab", None, None)
    return jax.shard_map(
        on_device, mesh=mesh, in_specs=in_specs, out_specs=out_specs, check_vma=False
    )
```
